32 devices in a mesh: groups: 2 (over x), gy: 16 (over z, y, core).
Axes of the slice: x: 2, y: 2, z: 4, core: 2. Of those that a mesh axis runs over, the one named last changes fastest.
Arguments:
- field: bfloat16 [64, 64, 2048], P(None, ('groups', 'gy')), parts along dimension 1, may hold values from -6 to 6
- cotangent: bfloat16 [64, 64, 2048], P(None, ('groups', 'gy')), parts along dimension 1, may hold values from -6 to 6
- banks: bfloat16 [2, 128, 36864], P(None, 'gy'), may hold values from -0.25 to 0.25
- region_map: int32 [64, 2048], P(('groups', 'gy')), parts along dimension 0, may hold values from 0 to 127, as said below
- tile_regions: int32 [512, 2], P(('groups', 'gy')), parts along dimension 0, may hold values from 0 to 127, as said below
- bank_slot: int32 [256], P('groups'), parts along dimension 0, may hold values from 0 to 127, as said below
Outputs:
- refined: bfloat16 [64, 64, 2048], P(None, ('groups', 'gy')), parts along dimension 1
- input_grad: bfloat16 [64, 64, 2048], P(None, ('groups', 'gy')), parts along dimension 1
- grad_banks: float32 [4, 128, 36864], P('groups', 'gy'), parts along dimension 0
The draws below stay inside these ranges and needn't reach their ends.
There are 2 independent parts, one for each index of `groups`. The reference program is written for one: setup_inputs(seed, part) draws one part's arguments, and reference() takes and returns one part's arrays. A program takes and returns all parts, laid end to end along the dimension named above; an argument that names none is the same for every part. Nothing has to cross between parts.
Inputs may be any that keep to these rules, and one draw needn't show every extreme that they name: `region_map`: the region of every cell is one of the two regions that tile_regions lists for its tile. `tile_regions`: the two regions of a tile differ; the 32 regions listed for the tiles of one group of 2 rows are distinct, at most 2 of them has bank rows in one aligned block of 8 rows of banks, and some block holds exactly 2 of them. `bank_slot`: A permutation.
All inputs are finite; a program needn't handle non-finite values.
Results may differ from the reference program's by a relative error of at most 0.0054.
Values may be sent and summed in bfloat16 or wider, within the bound.
No kernel may reach another device: no remote copies, remote signals or barrier semaphores. Data moves between devices by JAX's collectives and lax.ppermute only.
A program may use at most 128 MiB of HBM per device.

```python
import jax
import jax.numpy as jnp
from jax import lax

C = 64
ROWS_DEV = 2
BLOCK = 128
BANDS = 16
COLS = 2048
HEIGHT = 32
REG_ROWS = 8
REGIONS = 128
BANKS_DEV = 8
N_GY = 16


def layout(key):
    relabel = jax.random.permutation(jax.random.fold_in(key, 7001), REGIONS)
    holders = jax.random.permutation(jax.random.fold_in(key, 7002), N_GY)
    shifts = jax.random.randint(jax.random.fold_in(key, 7003), (COLS,), 0, 2 * ROWS_DEV)
    return (relabel.astype(jnp.int32), holders.astype(jnp.int32), shifts.astype(jnp.int32))


def draw_region_map(key, part):
    relabel, holders, shifts = layout(key)
    row_ids = jnp.arange(HEIGHT, dtype=jnp.int32)
    col_ids = jnp.arange(COLS, dtype=jnp.int32)
    band_ids = (row_ids[:, None] + shifts[None, :]) // (2 * ROWS_DEV) % REG_ROWS
    return relabel[band_ids * BANDS + (col_ids // BLOCK)[None, :]].astype(jnp.int32)


def draw_tile_regions(key, part):
    relabel, holders, shifts = layout(key)
    dev_ids = jnp.arange(N_GY, dtype=jnp.int32)
    col_ids = jnp.arange(BANDS, dtype=jnp.int32)
    lower = (dev_ids // 2)[:, None] * BANDS + col_ids[None, :]
    upper = ((dev_ids // 2 + 1) % REG_ROWS)[:, None] * BANDS + col_ids[None, :]
    stacked = jnp.stack([lower, upper], axis=-1).reshape(N_GY * BANDS, 2)
    return relabel[stacked].astype(jnp.int32)


def draw_bank_slot(key, part):
    relabel, holders, shifts = layout(key)
    region_ids = jnp.arange(REGIONS, dtype=jnp.int32)
    band_ids = region_ids // BANDS
    col_ids = region_ids % BANDS
    keyed = band_ids % 4 * BANDS + col_ids
    holder = holders[keyed % N_GY]
    local_row = band_ids // 4 * (4 * BANDS // N_GY) + keyed // N_GY
    slot_flat = holder * BANKS_DEV + local_row
    return jnp.zeros((REGIONS,), jnp.int32).at[relabel].set(slot_flat.astype(jnp.int32))


def block_levels(stream_key, dims, cuts, low, largest):
    gain, own = 1.0, jax.random.fold_in(stream_key, 6)
    for dim, shards_of in cuts:
        heights = jnp.exp(jax.random.uniform(jax.random.fold_in(own, dim), (shards_of,), jnp.float32, low / len(cuts), largest / len(cuts)))
        gain = gain * jnp.repeat(heights, dims[dim] // shards_of).reshape([-1 if axis == dim else 1 for axis in range(len(dims))])
    return gain


def gaussian(stream_key, dims, scale, bound, split=(), kind=jnp.bfloat16):
    level = block_levels(stream_key, dims, split, -0.22, 0.18) if split else 1.0
    array = jax.random.normal(stream_key, dims, jnp.float32) * scale * level
    return jnp.minimum(jnp.maximum(array, -bound), bound).astype(kind)


def setup_inputs(seed: int = 0, part: int = 0) -> dict:
    seeds = jax.random.split(jax.random.key(seed), 7)
    own_keys = jax.random.split(jax.random.fold_in(seeds[6], part), 7)
    return {
        "field": gaussian(own_keys[0], (C, HEIGHT, COLS), 1.0, 6.0, ((1, 16),)),
        "cotangent": gaussian(own_keys[1], (C, HEIGHT, COLS), 1.0, 6.0, ((1, 16),)),
        "banks": gaussian(seeds[2], (2, REGIONS, 9 * C * C), (9 * C) ** -0.5, 0.25, ((1, 16),)),
        "region_map": draw_region_map(jax.random.fold_in(jax.random.fold_in(seeds[6], part), 71), part),
        "tile_regions": draw_tile_regions(jax.random.fold_in(jax.random.fold_in(seeds[6], part), 71), part),
        "bank_slot": draw_bank_slot(jax.random.fold_in(jax.random.fold_in(seeds[6], part), 71), part),
    }


def unfold(padded, tile_rows, tile_cols):
    pieces = [padded[:, 1 + shift_y:1 + shift_y + tile_rows, 1 + shift_x:1 + shift_x + tile_cols] for shift_y in (-1, 0, 1) for shift_x in (-1, 0, 1)]
    return jnp.concatenate(pieces, axis=0)


def work_layout(kernels, channels):
    leading = kernels.shape[:-1]
    reshaped = jnp.moveaxis(kernels.reshape(leading + (9, channels, channels)), -3, -2)
    return reshaped.reshape(leading + (channels, 9 * channels))


def bank_layout(grads, channels):
    leading = grads.shape[:-2]
    reshaped = jnp.moveaxis(grads.reshape(leading + (channels, 9, channels)), -2, -3)
    return reshaped.reshape(leading + (9 * channels * channels,))


def reference(field, cotangent, banks, region_map, tile_regions, bank_slot):
    channels = field.shape[0]
    tile_rows = ROWS_DEV
    tile_cols = COLS
    region_lists = tile_regions.reshape(N_GY, BANDS, 2)
    cell_regions = region_map.reshape(N_GY, tile_rows, BANDS, BLOCK)
    list_by_slot = jnp.transpose(region_lists, (0, 2, 1))
    slot_masks = (cell_regions[:, None] == list_by_slot[:, :, None, :, None]).astype(jnp.float32)
    tile_ids = jnp.arange(N_GY, dtype=jnp.int32)

    def tile_weights(layer, tile):
        rows_of = bank_slot[region_lists[tile]]
        return work_layout(banks[layer][rows_of].astype(jnp.float32), channels)

    def tile_columns(act_pad, tile):
        window = lax.dynamic_slice_in_dim(act_pad, (tile * tile_rows).astype(jnp.int32), tile_rows + 2, axis=1)
        return unfold(window, tile_rows, tile_cols).reshape(9 * channels, tile_rows, BANDS, BLOCK).astype(jnp.float32)

    def to_whole(stacked):
        return jnp.moveaxis(stacked, 0, 1).reshape(channels, N_GY * tile_rows, tile_cols)

    def conv(activation, layer):
        act_pad = jnp.pad(activation, ((0, 0), (1, 1), (1, 1)))

        def one_tile(tile):
            columns = tile_columns(act_pad, tile)
            per_slot = jnp.einsum("bsoj,jybx->soybx", tile_weights(layer, tile), columns)
            mixed = jnp.sum(per_slot * slot_masks[tile][:, None], axis=0)
            return mixed.reshape(channels, tile_rows, tile_cols)

        return to_whole(lax.map(one_tile, tile_ids))

    def backward(upstream, activation, layer):
        act_pad = jnp.pad(activation, ((0, 0), (1, 1), (1, 1)))
        up_tiles = jnp.moveaxis(upstream.reshape(channels, N_GY, tile_rows, BANDS, BLOCK), 1, 0)

        def spread_of(tile):
            masked = up_tiles[tile].astype(jnp.float32)[None] * slot_masks[tile][:, None]
            spread = jnp.einsum("bsoj,soybx->jybx", tile_weights(layer, tile), masked).astype(jnp.bfloat16)
            return masked, spread.reshape(9, channels, tile_rows, tile_cols)

        def scan_step(accum, tile):
            masked, spread = spread_of(tile)
            columns = tile_columns(act_pad, tile)
            partial_value = jnp.einsum("soybx,jybx->bsoj", masked, columns)
            rounded = lax.optimization_barrier(bank_layout(partial_value, channels).astype(jnp.bfloat16))
            rows_of = bank_slot[region_lists[tile]].reshape(-1)
            accum = accum.at[rows_of].add(rounded.reshape(2 * BANDS, -1).astype(jnp.float32))
            return accum, (spread[0:3, :, 0, :], spread[6:9, :, tile_rows - 1, :])

        start = jnp.zeros((REGIONS, 9 * channels * channels), jnp.float32)
        grads, edges = lax.scan(scan_step, start, tile_ids)
        top_edges, bottom_edges = edges

        def one_tile(tile):
            ignored, spread = spread_of(tile)
            from_above = jnp.where(tile > 0, bottom_edges[jnp.maximum(tile - 1, 0)], jnp.zeros_like(bottom_edges[0]))
            from_below = jnp.where(tile < N_GY - 1, top_edges[jnp.minimum(tile + 1, N_GY - 1)], jnp.zeros_like(top_edges[0]))
            zero_rows = jnp.zeros((6, channels, tile_cols), jnp.bfloat16)
            top_row = jnp.concatenate([zero_rows, from_above], axis=0)
            bottom_row = jnp.concatenate([from_below, zero_rows], axis=0)
            extended = jnp.concatenate([top_row[:, :, None], spread, bottom_row[:, :, None]], axis=2)
            extended = jnp.pad(extended, ((0, 0), (0, 0), (0, 0), (1, 1)))
            total = jnp.zeros((channels, tile_rows, tile_cols), jnp.float32)
            for shift_y in (-1, 0, 1):
                for shift_x in (-1, 0, 1):
                    tap_idx = (shift_y + 1) * 3 + (shift_x + 1)
                    total = total + extended[tap_idx, :, 1 - shift_y:1 - shift_y + tile_rows, 1 - shift_x:1 - shift_x + tile_cols].astype(jnp.float32)
            return total

        return grads, to_whole(lax.map(one_tile, tile_ids))

    act0 = jnp.maximum(field, jnp.zeros((), jnp.bfloat16))
    hidden = (field.astype(jnp.float32) + conv(act0, 0)).astype(jnp.bfloat16)
    act1 = jnp.maximum(hidden, jnp.zeros((), jnp.bfloat16))
    refined = (hidden.astype(jnp.float32) + conv(act1, 1)).astype(jnp.bfloat16)
    grads_one, back_one = backward(cotangent, act1, 1)
    carried = (cotangent.astype(jnp.float32) + jnp.where(hidden > 0, back_one, jnp.zeros((), jnp.float32))).astype(jnp.bfloat16)
    grads_zero, back_zero = backward(carried, act0, 0)
    input_grad = (carried.astype(jnp.float32) + jnp.where(field > 0, back_zero, jnp.zeros((), jnp.float32))).astype(jnp.bfloat16)
    grad_banks = jnp.stack([grads_zero, grads_one]) * 0.03125
    return refined, input_grad, grad_banks
```

```python
import functools

import jax
import jax.numpy as jnp
from jax import lax
from jax.experimental import pallas as pl
from jax.experimental.pallas import tpu as pltpu
from jax.sharding import PartitionSpec as P

grad_unscale = 0.03125
F32 = jnp.float32
BF16 = jnp.bfloat16
LANES = 128
VMEM = pl.BlockSpec(memory_space=pltpu.VMEM)
SMEM = pl.BlockSpec(memory_space=pltpu.SMEM)
HBM = pl.BlockSpec(memory_space=pl.ANY)


def params(mib):
    return pltpu.CompilerParams(vmem_limit_bytes=mib * 2**20)


def cost(flops, moved):
    return pl.CostEstimate(flops=flops, bytes_accessed=moved, transcendentals=0)


def swap_halves(tile):
    return pltpu.roll(tile, LANES // 2, 1)


def low_half(tile):
    return lax.broadcasted_iota(jnp.int32, tile.shape, 1) < LANES // 2


def select_kernel(per_dev, rows, requested, banks, out, natural, travel, wire, sems):
    for chunk in range(rows):
        tile = banks[0, :, chunk * LANES : (chunk + 1) * LANES].astype(F32)
        natural[pl.ds(chunk, per_dev, stride=rows), :] = tile

    @pl.loop(0, per_dev)
    def _(row):
        base = row * rows

        def blend(first, second, start, count):
            even = jnp.where(low_half(first), first, swap_halves(second))
            odd = jnp.where(low_half(first), swap_halves(first), second)
            travel[pl.ds(start, count, stride=2), :] = even
            travel[pl.ds(start + 1, count, stride=2), :] = odd

        for pair in range(4):
            blend(
                natural[pl.ds(base + 64 * pair, 32), :],
                natural[pl.ds(base + 64 * pair + 32, 32), :],
                64 * pair,
                32,
            )
        blend(natural[pl.ds(base + 256, 16), :], natural[pl.ds(base + 272, 16), :], 256, 16)
        wire[row] = travel[...].astype(BF16)

    places = out.shape[0]

    def copy(place):
        source = wire.at[jnp.maximum(requested[place], 0)]
        return pltpu.make_async_copy(source, out.at[place], sems.at[place])

    for place in range(places):
        copy(place).start()
    for place in range(places):
        copy(place).wait()


def select(requested, banks, layer):
    layers, per_dev, width = banks.shape
    rows = width // LANES
    places = requested.shape[0]
    return pl.pallas_call(
        functools.partial(select_kernel, per_dev, rows),
        grid=(1,),
        out_shape=jax.ShapeDtypeStruct((places, rows, LANES), BF16),
        in_specs=[SMEM, pl.BlockSpec((1, per_dev, width), lambda step: (layer, 0, 0))],
        out_specs=HBM,
        scratch_shapes=[
            pltpu.VMEM((per_dev * rows, LANES), F32),
            pltpu.VMEM((rows, LANES), F32),
            pltpu.VMEM((per_dev, rows, LANES), BF16),
            pltpu.SemaphoreType.DMA((places,)),
        ],
        compiler_params=params(24),
        cost_estimate=cost(1000000, 2 * (places + per_dev) * width),
        name=f"select_{layer}",
    )(requested, banks)


def total_kernel(per_dev, rows, requested, parts, *rest):
    out, total, natural = rest[-3:]
    total[...] = jnp.zeros_like(total)

    @pl.loop(0, parts.shape[0])
    def _(place):
        row = requested[place]

        @pl.when(row >= 0)
        def _():
            total[pl.ds(pl.multiple_of(row * rows, 8), rows), :] += parts[place].astype(F32)

    @pl.loop(0, per_dev)
    def _(row):
        base = row * rows

        def split(start, count, first, second):
            even = total[pl.ds(base + start, count, stride=2), :] * grad_unscale
            odd = total[pl.ds(base + start + 1, count, stride=2), :] * grad_unscale
            natural[pl.ds(base + first, count), :] = jnp.where(low_half(even), even, swap_halves(odd))
            natural[pl.ds(base + second, count), :] = jnp.where(low_half(even), swap_halves(even), odd)

        for pair in range(4):
            split(64 * pair, 32, 64 * pair, 64 * pair + 32)
        split(256, 16, 256, 272)

    for chunk in range(rows):
        out[0, :, chunk * LANES : (chunk + 1) * LANES] = natural[pl.ds(chunk, per_dev, stride=rows), :]


def total_of(requested, parts, banks, layer, earlier=None):
    layers, per_dev, width = banks.shape
    rows = width // LANES
    places = requested.shape[0]
    args, specs = [requested, parts], [SMEM, pl.BlockSpec(parts.shape, lambda step: (0, 0, 0))]
    if earlier is not None:
        args.append(earlier)
        specs.append(HBM)
    return pl.pallas_call(
        functools.partial(total_kernel, per_dev, rows),
        grid=(1,),
        out_shape=jax.ShapeDtypeStruct((layers, per_dev, width), F32),
        in_specs=specs,
        out_specs=pl.BlockSpec((1, per_dev, width), lambda step: (layer, 0, 0)),
        scratch_shapes=[
            pltpu.VMEM((per_dev * rows, LANES), F32),
            pltpu.VMEM((per_dev * rows, LANES), F32),
        ],
        input_output_aliases={2: 0} if earlier is not None else {},
        compiler_params=params(32),
        cost_estimate=cost(1000000, 2 * places * width + 4 * per_dev * width),
        name=f"total_{layer}",
    )(*args)


def fill_shifts(above, middle, below, shifts):
    tile_rows, channels, columns = middle.shape
    step = 16

    @pl.loop(0, channels // step)
    def _(group):
        start = pl.multiple_of(group * step, step)
        for row in range(tile_rows + 2):
            if row == 0:
                cells = above[pl.ds(start, step), :]
            elif row == tile_rows + 1:
                cells = below[pl.ds(start, step), :]
            else:
                cells = middle[row - 1, pl.ds(start, step), :]
            cells = jnp.maximum(cells.astype(F32), 0.0)
            column = lax.broadcasted_iota(jnp.int32, cells.shape, 1)
            left = jnp.where(column == 0, 0.0, pltpu.roll(cells, 1, 1))
            right = jnp.where(column == columns - 1, 0.0, pltpu.roll(cells, columns - 1, 1))
            shifts[0, row, pl.ds(start, step), :] = left.astype(BF16)
            shifts[1, row, pl.ds(start, step), :] = cells.astype(BF16)
            shifts[2, row, pl.ds(start, step), :] = right.astype(BF16)


def band_slice(band):
    return pl.ds(pl.multiple_of(band * LANES, LANES), LANES)


def unfolded(shifts, band, tile_rows):
    taps = []
    for shift_y in range(3):
        for shift_x in range(3):
            rows = [shifts[shift_x, shift_y + row, :, band_slice(band)] for row in range(tile_rows)]
            taps.append(jnp.concatenate(rows, axis=1))
    return jnp.concatenate(taps, axis=0)


def band_weights(kernels, position, band):
    wide, last = [], []
    for slot in range(2):
        one = kernels.at[position[2 * band + slot]]
        wide.append(jnp.concatenate([one[64 * pair : 64 * pair + 64, :] for pair in range(4)], axis=1))
        tail = one[256:288, :]
        last.extend([tail[:, :64], tail[:, 64:]])
    return jnp.concatenate(wide, axis=0), jnp.concatenate(last, axis=0)


def first_mask(regions, listed, band, channels, tile_rows):
    rows = [regions[row : row + 1, band_slice(band)] for row in range(tile_rows)]
    flat = jnp.concatenate(rows, axis=1)
    return jnp.broadcast_to(flat, (channels, flat.shape[1])) == listed[2 * band]


def masked(upstream, mask):
    wide = upstream.astype(F32)
    first = jnp.where(mask, wide, 0.0).astype(BF16)
    second = jnp.where(mask, 0.0, wide).astype(BF16)
    return jnp.concatenate([first, second], axis=0)


def side_by_side(cells, band, tile_rows):
    return jnp.concatenate([cells[row, :, band_slice(band)] for row in range(tile_rows)], axis=1)


def dot(left, right, left_dim, right_dim):
    return lax.dot_general(
        left, right, (((left_dim,), (right_dim,)), ((), ())), preferred_element_type=F32
    )


def conv_kernel(position, listed, regions, above, middle, below, kernels, out, shifts):
    tile_rows, channels, columns = middle.shape
    fill_shifts(above, middle, below, shifts)

    @pl.loop(0, columns // LANES)
    def _(band):
        cells = unfolded(shifts, band, tile_rows)
        wide, last = band_weights(kernels, position, band)
        both = dot(wide, cells[:512], 1, 0) + dot(last, cells[512:], 1, 0)
        mask = first_mask(regions, listed, band, channels, tile_rows)
        mixed = jnp.where(mask, both[:channels], both[channels:])
        for row in range(tile_rows):
            here = mixed[:, row * LANES : (row + 1) * LANES]
            here = here + middle[row, :, band_slice(band)].astype(F32)
            out[row, :, band_slice(band)] = here.astype(BF16)


def conv(position, listed, regions, above, middle, below, kernels, name):
    tile_rows, channels, columns = middle.shape
    return pl.pallas_call(
        conv_kernel,
        out_shape=jax.ShapeDtypeStruct(middle.shape, BF16),
        in_specs=[SMEM, SMEM] + [VMEM] * 5,
        out_specs=VMEM,
        scratch_shapes=[pltpu.VMEM((3, tile_rows + 2, channels, columns), BF16)],
        compiler_params=params(32),
        cost_estimate=cost(4 * 9 * channels * channels * columns * tile_rows, 5000000),
        name=name,
    )(position, listed, regions, above, middle, below, kernels)


def partial_bands(position, listed, regions, upstream, shifts, out):
    tile_rows, channels, columns = upstream.shape

    @pl.loop(0, columns // LANES)
    def _(band):
        cells = unfolded(shifts, band, tile_rows)
        mask = first_mask(regions, listed, band, channels, tile_rows)
        both = masked(side_by_side(upstream, band, tile_rows), mask)
        sums = dot(both, cells, 1, 1).astype(BF16)
        for slot in range(2):
            mine = sums[channels * slot : channels * (slot + 1)]
            there = out.at[position[2 * band + slot]]
            for pair in range(4):
                there[64 * pair : 64 * pair + 64, :] = mine[:, LANES * pair : LANES * (pair + 1)]
            there[256:288, :] = jnp.concatenate([mine[:32, 512:], mine[32:, 512:]], axis=1)


def partial_kernel(position, listed, regions, upstream, above, middle, below, out, shifts):
    fill_shifts(above, middle, below, shifts)
    partial_bands(position, listed, regions, upstream, shifts, out)


def partial_of(position, listed, regions, upstream, above, middle, below, places):
    tile_rows, channels, columns = middle.shape
    rows = 9 * channels * channels // LANES
    return pl.pallas_call(
        partial_kernel,
        out_shape=jax.ShapeDtypeStruct((places, rows, LANES), BF16),
        in_specs=[SMEM, SMEM] + [VMEM] * 5,
        out_specs=VMEM,
        scratch_shapes=[pltpu.VMEM((3, tile_rows + 2, channels, columns), BF16)],
        compiler_params=params(32),
        cost_estimate=cost(4 * 9 * channels * channels * columns * tile_rows, 5000000),
        name="partial_1",
    )(position, listed, regions, upstream, above, middle, below)


def carried_kernel(
    position, listed, regions, cotangent, hidden, inner, from_above, from_below, above, middle, below,
    carried, out, shifts,
):
    tile_rows, channels, columns = middle.shape
    fill_shifts(above, middle, below, shifts)
    step = 16

    @pl.loop(0, channels // step)
    def _(group):
        here = pl.ds(pl.multiple_of(group * step, step), step)
        for row in range(tile_rows):
            back = inner[row, here, :]
            if row == 0:
                back = back + from_above[here, :].astype(F32)
            if row == tile_rows - 1:
                back = back + from_below[here, :].astype(F32)
            keep = hidden[row, here, :].astype(F32) > 0.0
            value = cotangent[row, here, :].astype(F32) + jnp.where(keep, back, 0.0)
            carried[row, here, :] = value.astype(BF16)

    partial_bands(position, listed, regions, carried, shifts, out)


def carried_of(
    position, listed, regions, cotangent, hidden, inner, from_above, from_below, above, middle, below,
    places,
):
    tile_rows, channels, columns = middle.shape
    rows = 9 * channels * channels // LANES
    return pl.pallas_call(
        carried_kernel,
        out_shape=(
            jax.ShapeDtypeStruct(middle.shape, BF16),
            jax.ShapeDtypeStruct((places, rows, LANES), BF16),
        ),
        in_specs=[SMEM, SMEM] + [VMEM] * 9,
        out_specs=(VMEM, VMEM),
        scratch_shapes=[pltpu.VMEM((3, tile_rows + 2, channels, columns), BF16)],
        compiler_params=params(32),
        cost_estimate=cost(4 * 9 * channels * channels * columns * tile_rows, 7000000),
        name="carried_partial_0",
    )(
        position, listed, regions, cotangent, hidden, inner, from_above, from_below, above, middle,
        below,
    )


def spread_kernel(position, listed, regions, upstream, kernels, inner, edges, total):
    tile_rows, channels, columns = upstream.shape
    total[...] = jnp.zeros_like(total)

    @pl.loop(0, columns // LANES)
    def _(band):
        wide, last = band_weights(kernels, position, band)
        mask = first_mask(regions, listed, band, channels, tile_rows)
        both = masked(side_by_side(upstream, band, tile_rows), mask)
        spread = jnp.concatenate([dot(wide, both, 0, 0), dot(last, both, 0, 0)], axis=0)
        lane = lax.broadcasted_iota(jnp.int32, (channels, LANES), 1)
        for target in range(tile_rows + 2):
            moved = []
            for shift_x in range(3):
                value = None
                for row in range(tile_rows):
                    shift_y = target - 1 - row + 1
                    if 0 <= shift_y <= 2:
                        tap = 3 * shift_y + shift_x
                        piece = spread[
                            channels * tap : channels * (tap + 1), LANES * row : LANES * (row + 1)
                        ]
                        value = piece if value is None else value + piece
                moved.append(value)
            left = pltpu.roll(moved[0], LANES - 1, 1)
            right = pltpu.roll(moved[2], 1, 1)
            centre = (
                moved[1]
                + jnp.where(lane == LANES - 1, 0.0, left)
                + jnp.where(lane == 0, 0.0, right)
            )
            total[target, :, band_slice(band)] += jnp.where(lane == LANES - 1, left, 0.0)
            total[target, :, band_slice(band + 1)] += centre
            total[target, :, band_slice(band + 2)] += jnp.where(lane == 0, right, 0.0)

    for row in range(tile_rows):
        inner[row] = total[row + 1, :, LANES : LANES + columns]
    edges[0] = total[0, :, LANES : LANES + columns].astype(BF16)
    edges[1] = total[tile_rows + 1, :, LANES : LANES + columns].astype(BF16)


def spread_of(position, listed, regions, upstream, kernels, name):
    tile_rows, channels, columns = upstream.shape
    return pl.pallas_call(
        spread_kernel,
        out_shape=(
            jax.ShapeDtypeStruct(upstream.shape, F32),
            jax.ShapeDtypeStruct((2, channels, columns), BF16),
        ),
        in_specs=[SMEM, SMEM] + [VMEM] * 3,
        out_specs=(VMEM, VMEM),
        scratch_shapes=[pltpu.VMEM((tile_rows + 2, channels, columns + 2 * LANES), F32)],
        compiler_params=params(32),
        cost_estimate=cost(4 * 9 * channels * channels * columns * tile_rows, 5000000),
        name=name,
    )(position, listed, regions, upstream, kernels)


def from_neighbours(upper, lower):
    count = lax.axis_size("gy")
    above = lax.ppermute(upper, "gy", [(i, i + 1) for i in range(count - 1)])
    below = lax.ppermute(lower, "gy", [(i + 1, i) for i in range(count - 1)])
    return above, below


def body(field, cotangent, banks, region_map, tile_regions, bank_slot):
    col_bands = tile_regions.shape[0]
    devices = lax.axis_size("gy")
    per_dev = banks.shape[1]
    slots_per = max(1, 2 * col_bands // devices)
    places = devices * slots_per
    listed = tile_regions.reshape(-1)
    bank_row = bank_slot[listed]
    holder = bank_row // per_dev
    local_row = bank_row % per_dev
    order = jnp.arange(2 * col_bands, dtype=jnp.int32)
    earlier = (holder[:, None] == holder[None, :]) & (order[None, :] < order[:, None])
    rank_in = jnp.sum(earlier.astype(jnp.int32), axis=-1)
    position = holder * slots_per + rank_in
    hits = position[None, :] == jnp.arange(places, dtype=jnp.int32)[:, None]
    wanted = jnp.max(jnp.where(hits, local_row[None, :], -1), axis=1).reshape(devices, slots_per)
    requested = lax.all_to_all(wanted, "gy", split_axis=0, concat_axis=0, tiled=True).reshape(-1)

    def exchange(value):
        return lax.all_to_all(value, "gy", split_axis=0, concat_axis=0, tiled=True)

    cells = jnp.transpose(field, (1, 0, 2))
    upstream = jnp.transpose(cotangent, (1, 0, 2))
    last = cells.shape[0] - 1

    kernel_zero = exchange(select(requested, banks, 0))
    kernel_one = exchange(select(requested, banks, 1))
    above, below = from_neighbours(cells[last], cells[0])
    where = (position, listed, region_map)
    hidden = conv(*where, above, cells, below, kernel_zero, "conv_0")
    hidden_above, hidden_below = from_neighbours(hidden[last], hidden[0])
    around = (hidden_above, hidden, hidden_below)
    sent_one = exchange(partial_of(*where, upstream, *around, places))
    inner_one, edges_one = spread_of(*where, upstream, kernel_one, "spread_1")
    from_above, from_below = from_neighbours(edges_one[1], edges_one[0])
    refined = conv(*where, *around, kernel_one, "conv_1")
    carried, partial_zero = carried_of(
        *where, upstream, hidden, inner_one, from_above, from_below, above, cells, below, places
    )
    sent_zero = exchange(partial_zero)
    inner_zero, edges_zero = spread_of(*where, carried, kernel_zero, "spread_0")
    from_above, from_below = from_neighbours(edges_zero[1], edges_zero[0])
    back = inner_zero.at[0].add(from_above.astype(F32)).at[last].add(from_below.astype(F32))
    input_grad = (carried.astype(F32) + jnp.where(cells > 0, back, 0.0)).astype(BF16)
    half = total_of(requested, sent_one, banks, 1)
    grad_banks = total_of(requested, sent_zero, banks, 0, half)
    return (jnp.transpose(refined, (1, 0, 2)), jnp.transpose(input_grad, (1, 0, 2)), grad_banks)


def solution(mesh):
    return jax.shard_map(
        body,
        mesh=mesh,
        in_specs=(
            P(None, ("groups", "gy"), None),
            P(None, ("groups", "gy"), None),
            P(None, "gy", None),
            P(("groups", "gy"), None),
            P(("groups", "gy"), None),
            P("groups"),
        ),
        out_specs=(
            P(None, ("groups", "gy"), None),
            P(None, ("groups", "gy"), None),
            P("groups", "gy", None),
        ),
        check_vma=False,
    )
```

```python
import functools

import jax
import jax.numpy as jnp
from jax import lax
from jax.experimental import pallas as pl
from jax.experimental.pallas import tpu as pltpu
from jax.sharding import PartitionSpec as P

grad_unscale = 0.03125
F32 = jnp.float32
BF16 = jnp.bfloat16
LANES = 128
VMEM = pl.BlockSpec(memory_space=pltpu.VMEM)
SMEM = pl.BlockSpec(memory_space=pltpu.SMEM)
HBM = pl.BlockSpec(memory_space=pl.ANY)


def params(mib):
    return pltpu.CompilerParams(vmem_limit_bytes=mib * 2**20)


def cost(flops, moved):
    return pl.CostEstimate(flops=flops, bytes_accessed=moved, transcendentals=0)


def swap_halves(tile):
    return pltpu.roll(tile, LANES // 2, 1)


def low_half(tile):
    return lax.broadcasted_iota(jnp.int32, tile.shape, 1) < LANES // 2


def select_kernel(per_dev, rows, requested, banks, out, natural, travel, wire, sems):
    for chunk in range(rows):
        tile = banks[0, :, chunk * LANES : (chunk + 1) * LANES].astype(F32)
        natural[pl.ds(chunk, per_dev, stride=rows), :] = tile

    @pl.loop(0, per_dev)
    def _(row):
        base = row * rows

        def blend(first, second, start, count):
            even = jnp.where(low_half(first), first, swap_halves(second))
            odd = jnp.where(low_half(first), swap_halves(first), second)
            travel[pl.ds(start, count, stride=2), :] = even
            travel[pl.ds(start + 1, count, stride=2), :] = odd

        for pair in range(4):
            blend(
                natural[pl.ds(base + 64 * pair, 32), :],
                natural[pl.ds(base + 64 * pair + 32, 32), :],
                64 * pair,
                32,
            )
        blend(natural[pl.ds(base + 256, 16), :], natural[pl.ds(base + 272, 16), :], 256, 16)
        wire[row] = travel[...].astype(BF16)

    places = out.shape[0]

    def copy(place):
        source = wire.at[jnp.maximum(requested[place], 0)]
        return pltpu.make_async_copy(source, out.at[place], sems.at[place])

    for place in range(places):
        copy(place).start()
    for place in range(places):
        copy(place).wait()


def select(requested, banks, layer):
    layers, per_dev, width = banks.shape
    rows = width // LANES
    places = requested.shape[0]
    return pl.pallas_call(
        functools.partial(select_kernel, per_dev, rows),
        grid=(1,),
        out_shape=jax.ShapeDtypeStruct((places, rows, LANES), BF16),
        in_specs=[SMEM, pl.BlockSpec((1, per_dev, width), lambda step: (layer, 0, 0))],
        out_specs=HBM,
        scratch_shapes=[
            pltpu.VMEM((per_dev * rows, LANES), F32),
            pltpu.VMEM((rows, LANES), F32),
            pltpu.VMEM((per_dev, rows, LANES), BF16),
            pltpu.SemaphoreType.DMA((places,)),
        ],
        compiler_params=params(24),
        cost_estimate=cost(1000000, 2 * (places + per_dev) * width),
        name=f"select_{layer}",
    )(requested, banks)


def total_kernel(per_dev, rows, requested, parts, *rest):
    out, total, natural = rest[-3:]
    total[...] = jnp.zeros_like(total)

    @pl.loop(0, parts.shape[0])
    def _(place):
        row = requested[place]

        @pl.when(row >= 0)
        def _():
            total[pl.ds(pl.multiple_of(row * rows, 8), rows), :] += parts[place].astype(F32)

    @pl.loop(0, per_dev)
    def _(row):
        base = row * rows

        def split(start, count, first, second):
            even = total[pl.ds(base + start, count, stride=2), :] * grad_unscale
            odd = total[pl.ds(base + start + 1, count, stride=2), :] * grad_unscale
            natural[pl.ds(base + first, count), :] = jnp.where(low_half(even), even, swap_halves(odd))
            natural[pl.ds(base + second, count), :] = jnp.where(low_half(even), swap_halves(even), odd)

        for pair in range(4):
            split(64 * pair, 32, 64 * pair, 64 * pair + 32)
        split(256, 16, 256, 272)

    for chunk in range(rows):
        out[0, :, chunk * LANES : (chunk + 1) * LANES] = natural[pl.ds(chunk, per_dev, stride=rows), :]


def total_of(requested, parts, banks, layer, earlier=None):
    layers, per_dev, width = banks.shape
    rows = width // LANES
    places = requested.shape[0]
    args, specs = [requested, parts], [SMEM, pl.BlockSpec(parts.shape, lambda step: (0, 0, 0))]
    if earlier is not None:
        args.append(earlier)
        specs.append(HBM)
    return pl.pallas_call(
        functools.partial(total_kernel, per_dev, rows),
        grid=(1,),
        out_shape=jax.ShapeDtypeStruct((layers, per_dev, width), F32),
        in_specs=specs,
        out_specs=pl.BlockSpec((1, per_dev, width), lambda step: (layer, 0, 0)),
        scratch_shapes=[
            pltpu.VMEM((per_dev * rows, LANES), F32),
            pltpu.VMEM((per_dev * rows, LANES), F32),
        ],
        input_output_aliases={2: 0} if earlier is not None else {},
        compiler_params=params(32),
        cost_estimate=cost(1000000, 2 * places * width + 4 * per_dev * width),
        name=f"total_{layer}",
    )(*args)


def fill_shifts(above, middle, below, shifts):
    tile_rows, channels, columns = middle.shape
    step = 16

    @pl.loop(0, channels // step)
    def _(group):
        start = pl.multiple_of(group * step, step)
        for row in range(tile_rows + 2):
            if row == 0:
                cells = above[pl.ds(start, step), :]
            elif row == tile_rows + 1:
                cells = below[pl.ds(start, step), :]
            else:
                cells = middle[row - 1, pl.ds(start, step), :]
            cells = jnp.maximum(cells.astype(F32), 0.0)
            column = lax.broadcasted_iota(jnp.int32, cells.shape, 1)
            left = jnp.where(column == 0, 0.0, pltpu.roll(cells, 1, 1))
            right = jnp.where(column == columns - 1, 0.0, pltpu.roll(cells, columns - 1, 1))
            shifts[0, row, pl.ds(start, step), :] = left.astype(BF16)
            shifts[1, row, pl.ds(start, step), :] = cells.astype(BF16)
            shifts[2, row, pl.ds(start, step), :] = right.astype(BF16)


def band_slice(band):
    return pl.ds(pl.multiple_of(band * LANES, LANES), LANES)


def unfolded(shifts, band, tile_rows):
    taps = []
    for shift_y in range(3):
        for shift_x in range(3):
            rows = [shifts[shift_x, shift_y + row, :, band_slice(band)] for row in range(tile_rows)]
            taps.append(jnp.concatenate(rows, axis=1))
    return jnp.concatenate(taps, axis=0)


def band_weights(kernels, position, band):
    wide, last = [], []
    for slot in range(2):
        one = kernels.at[position[2 * band + slot]]
        wide.append(jnp.concatenate([one[64 * pair : 64 * pair + 64, :] for pair in range(4)], axis=1))
        tail = one[256:288, :]
        last.extend([tail[:, :64], tail[:, 64:]])
    return jnp.concatenate(wide, axis=0), jnp.concatenate(last, axis=0)


def first_mask(regions, listed, band, channels, tile_rows):
    rows = [regions[row : row + 1, band_slice(band)] for row in range(tile_rows)]
    flat = jnp.concatenate(rows, axis=1)
    return jnp.broadcast_to(flat, (channels, flat.shape[1])) == listed[2 * band]


def masked(upstream, mask):
    wide = upstream.astype(F32)
    first = jnp.where(mask, wide, 0.0).astype(BF16)
    second = jnp.where(mask, 0.0, wide).astype(BF16)
    return jnp.concatenate([first, second], axis=0)


def side_by_side(cells, band, tile_rows):
    return jnp.concatenate([cells[row, :, band_slice(band)] for row in range(tile_rows)], axis=1)


def dot(left, right, left_dim, right_dim):
    return lax.dot_general(
        left, right, (((left_dim,), (right_dim,)), ((), ())), preferred_element_type=F32
    )


def conv_kernel(position, listed, regions, above, middle, below, kernels, out, shifts):
    tile_rows, channels, columns = middle.shape
    fill_shifts(above, middle, below, shifts)

    @pl.loop(0, columns // LANES)
    def _(band):
        cells = unfolded(shifts, band, tile_rows)
        wide, last = band_weights(kernels, position, band)
        both = dot(wide, cells[:512], 1, 0) + dot(last, cells[512:], 1, 0)
        mask = first_mask(regions, listed, band, channels, tile_rows)
        mixed = jnp.where(mask, both[:channels], both[channels:])
        for row in range(tile_rows):
            here = mixed[:, row * LANES : (row + 1) * LANES]
            here = here + middle[row, :, band_slice(band)].astype(F32)
            out[row, :, band_slice(band)] = here.astype(BF16)


def conv(position, listed, regions, above, middle, below, kernels, name):
    tile_rows, channels, columns = middle.shape
    return pl.pallas_call(
        conv_kernel,
        out_shape=jax.ShapeDtypeStruct(middle.shape, BF16),
        in_specs=[SMEM, SMEM] + [VMEM] * 5,
        out_specs=VMEM,
        scratch_shapes=[pltpu.VMEM((3, tile_rows + 2, channels, columns), BF16)],
        compiler_params=params(32),
        cost_estimate=cost(4 * 9 * channels * channels * columns * tile_rows, 5000000),
        name=name,
    )(position, listed, regions, above, middle, below, kernels)


def partial_bands(position, listed, regions, upstream, shifts, out):
    tile_rows, channels, columns = upstream.shape

    @pl.loop(0, columns // LANES)
    def _(band):
        cells = unfolded(shifts, band, tile_rows)
        mask = first_mask(regions, listed, band, channels, tile_rows)
        both = masked(side_by_side(upstream, band, tile_rows), mask)
        sums = dot(both, cells, 1, 1).astype(BF16)
        for slot in range(2):
            mine = sums[channels * slot : channels * (slot + 1)]
            there = out.at[position[2 * band + slot]]
            for pair in range(4):
                there[64 * pair : 64 * pair + 64, :] = mine[:, LANES * pair : LANES * (pair + 1)]
            there[256:288, :] = jnp.concatenate([mine[:32, 512:], mine[32:, 512:]], axis=1)


def partial_kernel(position, listed, regions, upstream, above, middle, below, out, shifts):
    fill_shifts(above, middle, below, shifts)
    partial_bands(position, listed, regions, upstream, shifts, out)


def partial_of(position, listed, regions, upstream, above, middle, below, places):
    tile_rows, channels, columns = middle.shape
    rows = 9 * channels * channels // LANES
    return pl.pallas_call(
        partial_kernel,
        out_shape=jax.ShapeDtypeStruct((places, rows, LANES), BF16),
        in_specs=[SMEM, SMEM] + [VMEM] * 5,
        out_specs=VMEM,
        scratch_shapes=[pltpu.VMEM((3, tile_rows + 2, channels, columns), BF16)],
        compiler_params=params(32),
        cost_estimate=cost(4 * 9 * channels * channels * columns * tile_rows, 5000000),
        name="partial_1",
    )(position, listed, regions, upstream, above, middle, below)


def carried_kernel(
    position, listed, regions, cotangent, hidden, inner, from_above, from_below, above, middle, below,
    carried, out, shifts,
):
    tile_rows, channels, columns = middle.shape
    fill_shifts(above, middle, below, shifts)
    step = 16

    @pl.loop(0, channels // step)
    def _(group):
        here = pl.ds(pl.multiple_of(group * step, step), step)
        for row in range(tile_rows):
            back = inner[row, here, :]
            if row == 0:
                back = back + from_above[here, :].astype(F32)
            if row == tile_rows - 1:
                back = back + from_below[here, :].astype(F32)
            keep = hidden[row, here, :].astype(F32) > 0.0
            value = cotangent[row, here, :].astype(F32) + jnp.where(keep, back, 0.0)
            carried[row, here, :] = value.astype(BF16)

    partial_bands(position, listed, regions, carried, shifts, out)


def carried_of(
    position, listed, regions, cotangent, hidden, inner, from_above, from_below, above, middle, below,
    places,
):
    tile_rows, channels, columns = middle.shape
    rows = 9 * channels * channels // LANES
    return pl.pallas_call(
        carried_kernel,
        out_shape=(
            jax.ShapeDtypeStruct(middle.shape, BF16),
            jax.ShapeDtypeStruct((places, rows, LANES), BF16),
        ),
        in_specs=[SMEM, SMEM] + [VMEM] * 9,
        out_specs=(VMEM, VMEM),
        scratch_shapes=[pltpu.VMEM((3, tile_rows + 2, channels, columns), BF16)],
        compiler_params=params(32),
        cost_estimate=cost(4 * 9 * channels * channels * columns * tile_rows, 7000000),
        name="carried_partial_0",
    )(
        position, listed, regions, cotangent, hidden, inner, from_above, from_below, above, middle,
        below,
    )


def spread_kernel(position, listed, regions, upstream, kernels, inner, edges, total):
    tile_rows, channels, columns = upstream.shape
    total[...] = jnp.zeros_like(total)

    @pl.loop(0, columns // LANES)
    def _(band):
        wide, last = band_weights(kernels, position, band)
        mask = first_mask(regions, listed, band, channels, tile_rows)
        both = masked(side_by_side(upstream, band, tile_rows), mask)
        spread = jnp.concatenate([dot(wide, both, 0, 0), dot(last, both, 0, 0)], axis=0)
        lane = lax.broadcasted_iota(jnp.int32, (channels, LANES), 1)
        for target in range(tile_rows + 2):
            moved = []
            for shift_x in range(3):
                value = None
                for row in range(tile_rows):
                    shift_y = target - 1 - row + 1
                    if 0 <= shift_y <= 2:
                        tap = 3 * shift_y + shift_x
                        piece = spread[
                            channels * tap : channels * (tap + 1), LANES * row : LANES * (row + 1)
                        ]
                        value = piece if value is None else value + piece
                moved.append(value)
            left = pltpu.roll(moved[0], LANES - 1, 1)
            right = pltpu.roll(moved[2], 1, 1)
            centre = (
                moved[1]
                + jnp.where(lane == LANES - 1, 0.0, left)
                + jnp.where(lane == 0, 0.0, right)
            )
            total[target, :, band_slice(band)] += jnp.where(lane == LANES - 1, left, 0.0)
            total[target, :, band_slice(band + 1)] += centre
            total[target, :, band_slice(band + 2)] += jnp.where(lane == 0, right, 0.0)

    for row in range(tile_rows):
        inner[row] = total[row + 1, :, LANES : LANES + columns]
    edges[0] = total[0, :, LANES : LANES + columns].astype(BF16)
    edges[1] = total[tile_rows + 1, :, LANES : LANES + columns].astype(BF16)


def spread_of(position, listed, regions, upstream, kernels, name):
    tile_rows, channels, columns = upstream.shape
    return pl.pallas_call(
        spread_kernel,
        out_shape=(
            jax.ShapeDtypeStruct(upstream.shape, F32),
            jax.ShapeDtypeStruct((2, channels, columns), BF16),
        ),
        in_specs=[SMEM, SMEM] + [VMEM] * 3,
        out_specs=(VMEM, VMEM),
        scratch_shapes=[pltpu.VMEM((tile_rows + 2, channels, columns + 2 * LANES), F32)],
        compiler_params=params(32),
        cost_estimate=cost(4 * 9 * channels * channels * columns * tile_rows, 5000000),
        name=name,
    )(position, listed, regions, upstream, kernels)


def from_neighbours(upper, lower):
    count = lax.axis_size("gy")
    above = lax.ppermute(upper, "gy", [(i, i + 1) for i in range(count - 1)])
    below = lax.ppermute(lower, "gy", [(i + 1, i) for i in range(count - 1)])
    return above, below


def after(first, value):
    return lax.optimization_barrier((*first, value))


def body(field, cotangent, banks, region_map, tile_regions, bank_slot):
    col_bands = tile_regions.shape[0]
    devices = lax.axis_size("gy")
    per_dev = banks.shape[1]
    slots_per = max(1, 2 * col_bands // devices)
    places = devices * slots_per
    listed = tile_regions.reshape(-1)
    bank_row = bank_slot[listed]
    holder = bank_row // per_dev
    local_row = bank_row % per_dev
    order = jnp.arange(2 * col_bands, dtype=jnp.int32)
    earlier = (holder[:, None] == holder[None, :]) & (order[None, :] < order[:, None])
    rank_in = jnp.sum(earlier.astype(jnp.int32), axis=-1)
    position = holder * slots_per + rank_in
    hits = position[None, :] == jnp.arange(places, dtype=jnp.int32)[:, None]
    wanted = jnp.max(jnp.where(hits, local_row[None, :], -1), axis=1).reshape(devices, slots_per)
    requested = lax.all_to_all(wanted, "gy", split_axis=0, concat_axis=0, tiled=True).reshape(-1)

    def exchange(value):
        return lax.all_to_all(value, "gy", split_axis=0, concat_axis=0, tiled=True)

    cells = jnp.transpose(field, (1, 0, 2))
    upstream = jnp.transpose(cotangent, (1, 0, 2))
    last = cells.shape[0] - 1

    where = (position, listed, region_map)
    above, below, requested = after(from_neighbours(cells[last], cells[0]), requested)
    wire_one = select(requested, banks, 1)
    wire_one, requested_then = after((wire_one,), requested)
    kernel_one = exchange(wire_one)
    kernel_zero = exchange(select(requested_then, banks, 0))
    inner_one, edges_one = spread_of(*where, upstream, kernel_one, "spread_1")
    from_above, from_below = from_neighbours(edges_one[1], edges_one[0])
    hidden = conv(*where, above, cells, below, kernel_zero, "conv_0")
    hidden_above, hidden_below = from_neighbours(hidden[last], hidden[0])
    carried, partial_zero = carried_of(
        *where, upstream, hidden, inner_one, from_above, from_below, above, cells, below, places
    )
    hidden_above, hidden_below, partial_zero = after((hidden_above, hidden_below), partial_zero)
    around = (hidden_above, hidden, hidden_below)
    sent_zero = exchange(partial_zero)
    inner_zero, edges_zero = spread_of(*where, carried, kernel_zero, "spread_0")
    from_above, from_below = from_neighbours(edges_zero[1], edges_zero[0])
    sent_one = exchange(partial_of(*where, upstream, *around, places))
    refined = conv(*where, *around, kernel_one, "conv_1")
    back = inner_zero.at[0].add(from_above.astype(F32)).at[last].add(from_below.astype(F32))
    input_grad = (carried.astype(F32) + jnp.where(cells > 0, back, 0.0)).astype(BF16)
    half = total_of(requested, sent_zero, banks, 0)
    grad_banks = total_of(requested, sent_one, banks, 1, half)
    return (jnp.transpose(refined, (1, 0, 2)), jnp.transpose(input_grad, (1, 0, 2)), grad_banks)


def solution(mesh):
    return jax.shard_map(
        body,
        mesh=mesh,
        in_specs=(
            P(None, ("groups", "gy"), None),
            P(None, ("groups", "gy"), None),
            P(None, "gy", None),
            P(("groups", "gy"), None),
            P(("groups", "gy"), None),
            P("groups"),
        ),
        out_specs=(
            P(None, ("groups", "gy"), None),
            P(None, ("groups", "gy"), None),
            P("groups", "gy", None),
        ),
        check_vma=False,
    )
```

```python
import functools

import jax
import jax.numpy as jnp
from jax import lax
from jax.experimental import pallas as pl
from jax.experimental.pallas import tpu as pltpu
from jax.sharding import Mesh
from jax.sharding import PartitionSpec as P

grad_unscale = 0.03125
F32 = jnp.float32
BF16 = jnp.bfloat16
LANES = 128
VMEM = pl.BlockSpec(memory_space=pltpu.VMEM)
SMEM = pl.BlockSpec(memory_space=pltpu.SMEM)
HBM = pl.BlockSpec(memory_space=pl.ANY)

NEAR = 4


def pairs_of(parts):
    return 4 // parts


def tail_of(parts):
    return 32 // parts


def part_rows(parts):
    return 64 * pairs_of(parts) + tail_of(parts)


def pair_start(pair, parts):
    return pair // pairs_of(parts) * part_rows(parts) + 64 * (pair % pairs_of(parts))


def tail_start(part, parts):
    return part * part_rows(parts) + 64 * pairs_of(parts)


def params(mib):
    return pltpu.CompilerParams(vmem_limit_bytes=mib * 2**20)


def cost(flops, moved):
    return pl.CostEstimate(flops=flops, bytes_accessed=moved, transcendentals=0)


def swap_halves(tile):
    return pltpu.roll(tile, LANES // 2, 1)


def low_half(tile):
    return lax.broadcasted_iota(jnp.int32, tile.shape, 1) < LANES // 2


def wire_kernel(parts, per_dev, rows, own_part, banks, out, natural, travel):
    for part in range(parts):

        @pl.when(own_part[0] == part)
        def _(part=part):
            pairs = range(part * pairs_of(parts), (part + 1) * pairs_of(parts))
            half = tail_of(parts) // 2
            for chunk in [*range(64 * pairs[0], 64 * pairs[-1] + 64), *range(256, rows)]:
                tile = banks[0, :, chunk * LANES : (chunk + 1) * LANES].astype(F32)
                natural[pl.ds(chunk, per_dev, stride=rows), :] = tile

            @pl.loop(0, per_dev)
            def _(row):
                base = row * rows

                def blend(first, second, start, count):
                    first = natural[pl.ds(base + first, count), :]
                    second = natural[pl.ds(base + second, count), :]
                    even = jnp.where(low_half(first), first, swap_halves(second))
                    odd = jnp.where(low_half(first), swap_halves(first), second)
                    travel[pl.ds(start, count, stride=2), :] = even
                    travel[pl.ds(start + 1, count, stride=2), :] = odd

                for order, pair in enumerate(pairs):
                    blend(64 * pair, 64 * pair + 32, 64 * order, 32)
                blend(256 + part * half, 272 + part * half, 64 * len(pairs), half)
                out[row] = travel[...].astype(BF16)


def wire(own_part, banks, layer, parts):
    layers, per_dev, width = banks.shape
    rows = width // LANES
    return pl.pallas_call(
        functools.partial(wire_kernel, parts, per_dev, rows),
        grid=(1,),
        out_shape=jax.ShapeDtypeStruct((per_dev, part_rows(parts), LANES), BF16),
        in_specs=[SMEM, pl.BlockSpec((1, per_dev, width), lambda step: (layer, 0, 0))],
        out_specs=pl.BlockSpec((per_dev, part_rows(parts), LANES), lambda step: (0, 0, 0)),
        scratch_shapes=[
            pltpu.VMEM((per_dev * rows, LANES), F32),
            pltpu.VMEM((part_rows(parts), LANES), F32),
        ],
        compiler_params=params(24),
        cost_estimate=cost(10**11, 4 * per_dev * width),
        name=f"wire_{layer}",
    )(own_part, banks)


def pack_kernel(step_of, row_of, *refs):
    buffers, out = refs[:-1], refs[-1]

    @pl.loop(0, out.shape[0])
    def _(place):
        for step, buffer in enumerate(buffers):

            @pl.when(step_of[place] == step)
            def _(buffer=buffer):
                out[place] = buffer[row_of[place]]


def pack(step_of, row_of, buffers, name):
    places = step_of.shape[0]
    shape = buffers[0].shape[1:]
    return pl.pallas_call(
        pack_kernel,
        out_shape=jax.ShapeDtypeStruct((places, *shape), BF16),
        in_specs=[SMEM, SMEM] + [VMEM] * len(buffers),
        out_specs=VMEM,
        compiler_params=params(32),
        cost_estimate=cost(10**11, 4 * places * shape[0] * shape[1]),
        name=name,
    )(step_of, row_of, *buffers)


def total_kernel(groups, per_dev, rows, requested, parts, *rest):
    out, total, natural = rest[-3:]
    total[...] = jnp.zeros_like(total)

    @pl.loop(0, parts.shape[0])
    def _(place):
        row = requested[place]

        @pl.when(row >= 0)
        def _():
            total[pl.ds(pl.multiple_of(row * rows, 8), rows), :] += parts[place].astype(F32)

    @pl.loop(0, per_dev)
    def _(row):
        base = row * rows

        def split(start, count, first, second):
            even = total[pl.ds(base + start, count, stride=2), :] * grad_unscale
            odd = total[pl.ds(base + start + 1, count, stride=2), :] * grad_unscale
            natural[pl.ds(base + first, count), :] = jnp.where(low_half(even), even, swap_halves(odd))
            natural[pl.ds(base + second, count), :] = jnp.where(low_half(even), swap_halves(even), odd)

        for pair in range(4):
            split(pair_start(pair, groups), 32, 64 * pair, 64 * pair + 32)
        half = tail_of(groups) // 2
        for part in range(groups):
            split(tail_start(part, groups), half, 256 + part * half, 272 + part * half)

    for chunk in range(rows):
        out[0, :, chunk * LANES : (chunk + 1) * LANES] = natural[pl.ds(chunk, per_dev, stride=rows), :]


def total_of(requested, parts, banks, layer, groups, earlier=None):
    layers, per_dev, width = banks.shape
    rows = width // LANES
    places = requested.shape[0]
    args, specs = [requested, parts], [SMEM, pl.BlockSpec(parts.shape, lambda step: (0, 0, 0))]
    if earlier is not None:
        args.append(earlier)
        specs.append(HBM)
    return pl.pallas_call(
        functools.partial(total_kernel, groups, per_dev, rows),
        grid=(1,),
        out_shape=jax.ShapeDtypeStruct((layers, per_dev, width), F32),
        in_specs=specs,
        out_specs=pl.BlockSpec((1, per_dev, width), lambda step: (layer, 0, 0)),
        scratch_shapes=[
            pltpu.VMEM((per_dev * rows, LANES), F32),
            pltpu.VMEM((per_dev * rows, LANES), F32),
        ],
        input_output_aliases={2: 0} if earlier is not None else {},
        compiler_params=params(32),
        cost_estimate=cost(1000000, 2 * places * width + 4 * per_dev * width),
        name=f"total_{layer}",
    )(*args)


def fill_shifts(above, middle, below, shifts):
    tile_rows, channels, columns = middle.shape
    step = 16

    @pl.loop(0, channels // step)
    def _(group):
        start = pl.multiple_of(group * step, step)
        for row in range(tile_rows + 2):
            if row == 0:
                cells = above[pl.ds(start, step), :]
            elif row == tile_rows + 1:
                cells = below[pl.ds(start, step), :]
            else:
                cells = middle[row - 1, pl.ds(start, step), :]
            cells = jnp.maximum(cells.astype(F32), 0.0)
            column = lax.broadcasted_iota(jnp.int32, cells.shape, 1)
            left = jnp.where(column == 0, 0.0, pltpu.roll(cells, 1, 1))
            right = jnp.where(column == columns - 1, 0.0, pltpu.roll(cells, columns - 1, 1))
            shifts[0, row, pl.ds(start, step), :] = left.astype(BF16)
            shifts[1, row, pl.ds(start, step), :] = cells.astype(BF16)
            shifts[2, row, pl.ds(start, step), :] = right.astype(BF16)


def band_slice(band):
    return pl.ds(pl.multiple_of(band * LANES, LANES), LANES)


def unfolded(shifts, band, tile_rows):
    taps = []
    for shift_y in range(3):
        for shift_x in range(3):
            rows = [shifts[shift_x, shift_y + row, :, band_slice(band)] for row in range(tile_rows)]
            taps.append(jnp.concatenate(rows, axis=1))
    return jnp.concatenate(taps, axis=0)


def band_weights(kernels, place_of, band):
    parts = kernels.shape[0]
    tail = 64 * pairs_of(parts)
    wide, last = [], []
    for slot in range(2):
        ones = [kernels.at[part, place_of[2 * band + slot]] for part in range(parts)]
        blocks = [one[start : start + 64, :] for one in ones for start in range(0, tail, 64)]
        wide.append(jnp.concatenate(blocks, axis=1))
        rest = jnp.concatenate([one[tail : tail + tail_of(parts), :] for one in ones], axis=0)
        last.extend([rest[:, :64], rest[:, 64:]])
    return jnp.concatenate(wide, axis=0), jnp.concatenate(last, axis=0)


def first_mask(regions, listed, band, channels, tile_rows):
    rows = [regions[row : row + 1, band_slice(band)] for row in range(tile_rows)]
    flat = jnp.concatenate(rows, axis=1)
    return jnp.broadcast_to(flat, (channels, flat.shape[1])) == listed[2 * band]


def masked(upstream, mask):
    wide = upstream.astype(F32)
    first = jnp.where(mask, wide, 0.0).astype(BF16)
    second = jnp.where(mask, 0.0, wide).astype(BF16)
    return jnp.concatenate([first, second], axis=0)


def side_by_side(cells, band, tile_rows):
    return jnp.concatenate([cells[row, :, band_slice(band)] for row in range(tile_rows)], axis=1)


def dot(left, right, left_dim, right_dim):
    return lax.dot_general(
        left, right, (((left_dim,), (right_dim,)), ((), ())), preferred_element_type=F32
    )


def conv_kernel(position, listed, regions, above, middle, below, kernels, out, shifts):
    tile_rows, channels, columns = middle.shape
    fill_shifts(above, middle, below, shifts)

    @pl.loop(0, columns // LANES, unroll=2)
    def _(band):
        cells = unfolded(shifts, band, tile_rows)
        wide, last = band_weights(kernels, position, band)
        both = dot(wide, cells[:512], 1, 0) + dot(last, cells[512:], 1, 0)
        mask = first_mask(regions, listed, band, channels, tile_rows)
        mixed = jnp.where(mask, both[:channels], both[channels:])
        for row in range(tile_rows):
            here = mixed[:, row * LANES : (row + 1) * LANES]
            here = here + middle[row, :, band_slice(band)].astype(F32)
            out[row, :, band_slice(band)] = here.astype(BF16)


def conv(position, listed, regions, above, middle, below, kernels, name):
    tile_rows, channels, columns = middle.shape
    return pl.pallas_call(
        conv_kernel,
        out_shape=jax.ShapeDtypeStruct(middle.shape, BF16),
        in_specs=[SMEM, SMEM] + [VMEM] * 5,
        out_specs=VMEM,
        scratch_shapes=[pltpu.VMEM((3, tile_rows + 2, channels, columns), BF16)],
        compiler_params=params(32),
        cost_estimate=cost(4 * 9 * channels * channels * columns * tile_rows, 5000000),
        name=name,
    )(position, listed, regions, above, middle, below, kernels)


def partial_bands(groups, position, listed, regions, upstream, shifts, out):
    tile_rows, channels, columns = upstream.shape

    @pl.loop(0, columns // LANES, unroll=2)
    def _(band):
        cells = unfolded(shifts, band, tile_rows)
        mask = first_mask(regions, listed, band, channels, tile_rows)
        both = masked(side_by_side(upstream, band, tile_rows), mask)
        sums = dot(both, cells, 1, 1).astype(BF16)
        for slot in range(2):
            mine = sums[channels * slot : channels * (slot + 1)]
            there = out.at[position[2 * band + slot]]
            for pair in range(4):
                start = pair_start(pair, groups)
                there[start : start + 64, :] = mine[:, LANES * pair : LANES * (pair + 1)]
            rest = jnp.concatenate([mine[:32, 512:], mine[32:, 512:]], axis=1)
            size = tail_of(groups)
            for part in range(groups):
                start = tail_start(part, groups)
                there[start : start + size, :] = rest[size * part : size * (part + 1)]


def partial_kernel(groups, position, listed, regions, upstream, above, middle, below, out, shifts):
    fill_shifts(above, middle, below, shifts)
    partial_bands(groups, position, listed, regions, upstream, shifts, out)


def partial_of(position, listed, regions, upstream, above, middle, below, places, groups):
    tile_rows, channels, columns = middle.shape
    rows = 9 * channels * channels // LANES
    return pl.pallas_call(
        functools.partial(partial_kernel, groups),
        out_shape=jax.ShapeDtypeStruct((places, rows, LANES), BF16),
        in_specs=[SMEM, SMEM] + [VMEM] * 5,
        out_specs=VMEM,
        scratch_shapes=[pltpu.VMEM((3, tile_rows + 2, channels, columns), BF16)],
        compiler_params=params(32),
        cost_estimate=cost(4 * 9 * channels * channels * columns * tile_rows, 5000000),
        name="partial_1",
    )(position, listed, regions, upstream, above, middle, below)


def carried_kernel(
    groups, position, listed, regions, cotangent, hidden, inner, from_above, from_below, above, middle, below,
    carried, out, shifts,
):
    tile_rows, channels, columns = middle.shape
    fill_shifts(above, middle, below, shifts)
    step = 16

    @pl.loop(0, channels // step)
    def _(group):
        here = pl.ds(pl.multiple_of(group * step, step), step)
        for row in range(tile_rows):
            back = inner[row, here, :]
            if row == 0:
                back = back + from_above[here, :].astype(F32)
            if row == tile_rows - 1:
                back = back + from_below[here, :].astype(F32)
            keep = hidden[row, here, :].astype(F32) > 0.0
            value = cotangent[row, here, :].astype(F32) + jnp.where(keep, back, 0.0)
            carried[row, here, :] = value.astype(BF16)

    partial_bands(groups, position, listed, regions, carried, shifts, out)


def carried_of(
    position, listed, regions, cotangent, hidden, inner, from_above, from_below, above, middle, below,
    places, groups,
):
    tile_rows, channels, columns = middle.shape
    rows = 9 * channels * channels // LANES
    return pl.pallas_call(
        functools.partial(carried_kernel, groups),
        out_shape=(
            jax.ShapeDtypeStruct(middle.shape, BF16),
            jax.ShapeDtypeStruct((places, rows, LANES), BF16),
        ),
        in_specs=[SMEM, SMEM] + [VMEM] * 9,
        out_specs=(VMEM, VMEM),
        scratch_shapes=[pltpu.VMEM((3, tile_rows + 2, channels, columns), BF16)],
        compiler_params=params(32),
        cost_estimate=cost(4 * 9 * channels * channels * columns * tile_rows, 7000000),
        name="carried_partial_0",
    )(
        position, listed, regions, cotangent, hidden, inner, from_above, from_below, above, middle,
        below,
    )


def spread_kernel(position, listed, regions, upstream, kernels, inner, edges, total):
    tile_rows, channels, columns = upstream.shape
    total[...] = jnp.zeros_like(total)

    @pl.loop(0, columns // LANES, unroll=2)
    def _(band):
        wide, last = band_weights(kernels, position, band)
        mask = first_mask(regions, listed, band, channels, tile_rows)
        both = masked(side_by_side(upstream, band, tile_rows), mask)
        spread = jnp.concatenate([dot(wide, both, 0, 0), dot(last, both, 0, 0)], axis=0)
        lane = lax.broadcasted_iota(jnp.int32, (channels, LANES), 1)
        for target in range(tile_rows + 2):
            moved = []
            for shift_x in range(3):
                value = None
                for row in range(tile_rows):
                    shift_y = target - 1 - row + 1
                    if 0 <= shift_y <= 2:
                        tap = 3 * shift_y + shift_x
                        piece = spread[
                            channels * tap : channels * (tap + 1), LANES * row : LANES * (row + 1)
                        ]
                        value = piece if value is None else value + piece
                moved.append(value)
            left = pltpu.roll(moved[0], LANES - 1, 1)
            right = pltpu.roll(moved[2], 1, 1)
            centre = (
                moved[1]
                + jnp.where(lane == LANES - 1, 0.0, left)
                + jnp.where(lane == 0, 0.0, right)
            )
            total[target, :, band_slice(band)] += jnp.where(lane == LANES - 1, left, 0.0)
            total[target, :, band_slice(band + 1)] += centre
            total[target, :, band_slice(band + 2)] += jnp.where(lane == 0, right, 0.0)

    for row in range(tile_rows):
        inner[row] = total[row + 1, :, LANES : LANES + columns]
    edges[0] = total[0, :, LANES : LANES + columns].astype(BF16)
    edges[1] = total[tile_rows + 1, :, LANES : LANES + columns].astype(BF16)


def spread_of(position, listed, regions, upstream, kernels, name):
    tile_rows, channels, columns = upstream.shape
    return pl.pallas_call(
        spread_kernel,
        out_shape=(
            jax.ShapeDtypeStruct(upstream.shape, F32),
            jax.ShapeDtypeStruct((2, channels, columns), BF16),
        ),
        in_specs=[SMEM, SMEM] + [VMEM] * 3,
        out_specs=(VMEM, VMEM),
        scratch_shapes=[pltpu.VMEM((tile_rows + 2, channels, columns + 2 * LANES), F32)],
        compiler_params=params(32),
        cost_estimate=cost(4 * 9 * channels * channels * columns * tile_rows, 5000000),
        name=name,
    )(position, listed, regions, upstream, kernels)


GY = ("far", "near")
PLANE = ("groups", "near")
ALL = ("groups", "far", "near")


def from_neighbours(upper, lower):
    count = lax.axis_size(GY)
    above = lax.ppermute(upper, GY, [(i, i + 1) for i in range(count - 1)])
    below = lax.ppermute(lower, GY, [(i + 1, i) for i in range(count - 1)])
    return above, below


def exchange(value, axes):
    return lax.all_to_all(value, axes, split_axis=0, concat_axis=0, tiled=True)


def after(first, value):
    return lax.optimization_barrier((*first, value))


def places_for(owner, owners, per_owner, content):
    order = jnp.arange(owner.shape[0], dtype=jnp.int32)
    earlier = (owner[:, None] == owner[None, :]) & (order[None, :] < order[:, None])
    position = owner * per_owner + jnp.sum(earlier.astype(jnp.int32), axis=-1)
    hits = position[None, :] == jnp.arange(owners * per_owner, dtype=jnp.int32)[:, None]
    wanted = jnp.max(jnp.where(hits, content[None, :], -1), axis=1)
    return position, wanted.reshape(owners, per_owner)


def body(field, cotangent, banks, region_map, tile_regions, bank_slot):
    col_bands = tile_regions.shape[0]
    groups, far, near = (lax.axis_size(axis) for axis in ALL)
    devices = far * near
    per_dev = banks.shape[1]
    slots_per = max(1, 2 * col_bands // devices)
    places = devices * slots_per
    most = min(far * slots_per, 2 * col_bands)
    listed = tile_regions.reshape(-1)
    bank_row = bank_slot[listed]
    holder = bank_row // per_dev
    local_row = bank_row % per_dev
    position, wanted = places_for(holder, devices, slots_per, local_row)
    source, asking = places_for(holder % near, near, most, holder // near * per_dev + local_row)
    my_group, my_far = lax.axis_index("groups"), lax.axis_index("far")

    cells = jnp.transpose(field, (1, 0, 2))
    upstream = jnp.transpose(cotangent, (1, 0, 2))
    last = cells.shape[0] - 1
    where = (position, listed, region_map)
    fetch = (source, listed, region_map)

    own_part = my_group.astype(jnp.int32).reshape(1)
    wire_one = wire(own_part, banks, 1, groups)
    turns = [[(k, (k + step) % far) for k in range(far)] for step in range(1, far)]
    bank_one = [wire_one] + [lax.ppermute(wire_one, "far", turn) for turn in turns]
    above, below = from_neighbours(cells[last], cells[0])
    *bank_one, above, below, own_part = after((*bank_one, above, below), own_part)
    wire_zero = wire(own_part, banks, 0, groups)
    bank_zero = [wire_zero] + [lax.ppermute(wire_zero, "far", turn) for turn in turns]
    message = jnp.concatenate(
        [
            jnp.broadcast_to(wanted.reshape(1, far, near, slots_per), (groups, far, near, slots_per)),
            jnp.broadcast_to(asking.reshape(1, 1, near, most), (groups, far, near, most)),
        ],
        axis=-1,
    )
    message = exchange(message.reshape(groups * devices, slots_per + most), ALL)
    message = message.reshape(groups, far, near, slots_per + most)
    requested = lax.dynamic_index_in_dim(message, my_group, 0, False)[:, :, :slots_per].reshape(-1)
    asked = lax.dynamic_index_in_dim(message, my_far, 1, False)[:, :, slots_per:].reshape(-1)
    step_of = jnp.where(asked < 0, 0, (my_far - asked // per_dev + far) % far).astype(jnp.int32)
    row_of = jnp.where(asked < 0, 0, asked % per_dev)

    def fetched(buffers, name):
        arrived = exchange(pack(step_of, row_of, buffers, name), PLANE)
        return arrived.reshape(groups, near * most, *arrived.shape[1:])

    kernel_one = fetched(bank_one, "pack_1")
    kernel_zero = fetched(bank_zero, "pack_0")
    inner_one, edges_one = spread_of(*fetch, upstream, kernel_one, "spread_1")
    from_above, from_below = from_neighbours(edges_one[1], edges_one[0])
    hidden = conv(*fetch, above, cells, below, kernel_zero, "conv_0")
    hidden_above, hidden_below = from_neighbours(hidden[last], hidden[0])
    carried, partial_zero = carried_of(
        *where, upstream, hidden, inner_one, from_above, from_below, above, cells, below, places, groups
    )
    hidden_above, hidden_below, partial_zero = after((hidden_above, hidden_below), partial_zero)
    around = (hidden_above, hidden, hidden_below)
    sent_zero = exchange(partial_zero, GY)
    inner_zero, edges_zero = spread_of(*fetch, carried, kernel_zero, "spread_0")
    from_above, from_below = from_neighbours(edges_zero[1], edges_zero[0])
    partial_one = partial_of(*where, upstream, *around, places, groups)
    from_above, from_below, partial_one = after((from_above, from_below), partial_one)
    sent_one = exchange(partial_one, GY)
    refined = conv(*fetch, *around, kernel_one, "conv_1")
    back = inner_zero.at[0].add(from_above.astype(F32)).at[last].add(from_below.astype(F32))
    input_grad = (carried.astype(F32) + jnp.where(cells > 0, back, 0.0)).astype(BF16)
    half = total_of(requested, sent_zero, banks, 0, groups)
    grad_banks = total_of(requested, sent_one, banks, 1, groups, half)
    return (jnp.transpose(refined, (1, 0, 2)), jnp.transpose(input_grad, (1, 0, 2)), grad_banks)


def solution(mesh):
    groups, devices = mesh.shape["groups"], mesh.shape["gy"]
    cut = Mesh(mesh.devices.reshape(groups, devices // NEAR, NEAR), ALL)
    return jax.shard_map(
        body,
        mesh=cut,
        in_specs=(
            P(None, ALL, None),
            P(None, ALL, None),
            P(None, GY, None),
            P(ALL, None),
            P(ALL, None),
            P("groups"),
        ),
        out_specs=(
            P(None, ALL, None),
            P(None, ALL, None),
            P("groups", GY, None),
        ),
        check_vma=False,
    )
```

```python
import functools

import jax
import jax.numpy as jnp
from jax import lax
from jax.experimental import pallas as pl
from jax.experimental.pallas import tpu as pltpu
from jax.sharding import Mesh
from jax.sharding import PartitionSpec as P

grad_unscale = 0.03125
F32 = jnp.float32
BF16 = jnp.bfloat16
LANES = 128
VMEM = pl.BlockSpec(memory_space=pltpu.VMEM)
SMEM = pl.BlockSpec(memory_space=pltpu.SMEM)
HBM = pl.BlockSpec(memory_space=pl.ANY)

NEAR = 4


def pairs_of(parts):
    return 4 // parts


def tail_of(parts):
    return 32 // parts


def part_rows(parts):
    return 64 * pairs_of(parts) + tail_of(parts)


def pair_start(pair, parts):
    return pair // pairs_of(parts) * part_rows(parts) + 64 * (pair % pairs_of(parts))


def tail_start(part, parts):
    return part * part_rows(parts) + 64 * pairs_of(parts)


def params(mib):
    return pltpu.CompilerParams(vmem_limit_bytes=mib * 2**20)


def cost(flops, moved):
    return pl.CostEstimate(flops=flops, bytes_accessed=moved, transcendentals=0)


def swap_halves(tile):
    return pltpu.roll(tile, LANES // 2, 1)


def low_half(tile):
    return lax.broadcasted_iota(jnp.int32, tile.shape, 1) < LANES // 2


def wire_kernel(parts, per_dev, rows, own_part, banks, *rest):
    outs, (natural, travel) = rest[:-2], rest[-2:]
    for part in range(parts):

        @pl.when(own_part[0] == part)
        def _(part=part):
            pairs = range(part * pairs_of(parts), (part + 1) * pairs_of(parts))
            half = tail_of(parts) // 2
            for chunk in [*range(64 * pairs[0], 64 * pairs[-1] + 64), *range(256, rows)]:
                tile = banks[0, :, chunk * LANES : (chunk + 1) * LANES].astype(F32)
                natural[pl.ds(chunk, per_dev, stride=rows), :] = tile

            @pl.loop(0, per_dev)
            def _(row):
                base = row * rows

                def blend(first, second, start, count):
                    first = natural[pl.ds(base + first, count), :]
                    second = natural[pl.ds(base + second, count), :]
                    even = jnp.where(low_half(first), first, swap_halves(second))
                    odd = jnp.where(low_half(first), swap_halves(first), second)
                    travel[pl.ds(start, count, stride=2), :] = even
                    travel[pl.ds(start + 1, count, stride=2), :] = odd

                for order, pair in enumerate(pairs):
                    blend(64 * pair, 64 * pair + 32, 64 * order, 32)
                blend(256 + part * half, 272 + part * half, 64 * len(pairs), half)
                start = 0
                for out in outs:
                    out[row] = travel[start : start + out.shape[1], :].astype(BF16)
                    start += out.shape[1]


def wire(own_part, banks, layer, parts, sizes):
    layers, per_dev, width = banks.shape
    rows = width // LANES
    return pl.pallas_call(
        functools.partial(wire_kernel, parts, per_dev, rows),
        grid=(1,),
        out_shape=[jax.ShapeDtypeStruct((per_dev, size, LANES), BF16) for size in sizes],
        in_specs=[SMEM, pl.BlockSpec((1, per_dev, width), lambda step: (layer, 0, 0))],
        out_specs=[pl.BlockSpec((per_dev, size, LANES), lambda step: (0, 0, 0)) for size in sizes],
        scratch_shapes=[
            pltpu.VMEM((per_dev * rows, LANES), F32),
            pltpu.VMEM((part_rows(parts), LANES), F32),
        ],
        compiler_params=params(24),
        cost_estimate=cost(10**6, 4 * per_dev * width),
        name=f"wire_{layer}",
    )(own_part, banks)


def pack_kernel(rows, *refs):
    buffers, out = refs[:-1], refs[-1]
    inner = rows.shape[1]
    slots = inner // len(buffers)

    @pl.loop(0, rows.shape[0])
    def _(target):
        for entry in range(inner):
            out[target * inner + entry] = buffers[entry // slots][rows[target, entry]]


def pack(rows, buffers, name):
    targets, inner = rows.shape
    shape = buffers[0].shape[1:]
    return pl.pallas_call(
        pack_kernel,
        out_shape=jax.ShapeDtypeStruct((targets * inner, *shape), BF16),
        in_specs=[SMEM] + [VMEM] * len(buffers),
        out_specs=VMEM,
        compiler_params=params(32),
        cost_estimate=cost(10**11, 4 * targets * inner * shape[0] * shape[1]),
        name=name,
    )(rows, *buffers)


def total_kernel(groups, per_dev, rows, requested, parts, *rest):
    out, total, natural = rest[-3:]
    total[...] = jnp.zeros_like(total)

    @pl.loop(0, parts.shape[0], unroll=4)
    def _(place):
        row = jnp.where(requested[place] < 0, per_dev, requested[place])
        total[pl.ds(pl.multiple_of(row * rows, 8), rows), :] += parts[place].astype(F32)

    @pl.loop(0, per_dev, unroll=2)
    def _(row):
        base = row * rows

        def split(start, count, first, second):
            even = total[pl.ds(base + start, count, stride=2), :] * grad_unscale
            odd = total[pl.ds(base + start + 1, count, stride=2), :] * grad_unscale
            natural[pl.ds(base + first, count), :] = jnp.where(low_half(even), even, swap_halves(odd))
            natural[pl.ds(base + second, count), :] = jnp.where(low_half(even), swap_halves(even), odd)

        for pair in range(4):
            split(pair_start(pair, groups), 32, 64 * pair, 64 * pair + 32)
        half = tail_of(groups) // 2
        for part in range(groups):
            split(tail_start(part, groups), half, 256 + part * half, 272 + part * half)

    for chunk in range(rows):
        out[0, :, chunk * LANES : (chunk + 1) * LANES] = natural[pl.ds(chunk, per_dev, stride=rows), :]


def total_of(requested, parts, banks, layer, groups, earlier=None):
    layers, per_dev, width = banks.shape
    rows = width // LANES
    places = requested.shape[0]
    args, specs = [requested, parts], [SMEM, pl.BlockSpec(parts.shape, lambda step: (0, 0, 0))]
    if earlier is not None:
        args.append(earlier)
        specs.append(HBM)
    return pl.pallas_call(
        functools.partial(total_kernel, groups, per_dev, rows),
        grid=(1,),
        out_shape=jax.ShapeDtypeStruct((layers, per_dev, width), F32),
        in_specs=specs,
        out_specs=pl.BlockSpec((1, per_dev, width), lambda step: (layer, 0, 0)),
        scratch_shapes=[
            pltpu.VMEM(((per_dev + 1) * rows, LANES), F32),
            pltpu.VMEM((per_dev * rows, LANES), F32),
        ],
        input_output_aliases={2: 0} if earlier is not None else {},
        compiler_params=params(32),
        cost_estimate=cost(1000000, 2 * places * width + 4 * per_dev * width),
        name=f"total_{layer}",
    )(*args)


def fill_shifts(above, middle, below, shifts):
    tile_rows, channels, columns = middle.shape
    step = 16

    @pl.loop(0, channels // step)
    def _(group):
        start = pl.multiple_of(group * step, step)
        for row in range(tile_rows + 2):
            if row == 0:
                cells = above[pl.ds(start, step), :]
            elif row == tile_rows + 1:
                cells = below[pl.ds(start, step), :]
            else:
                cells = middle[row - 1, pl.ds(start, step), :]
            cells = jnp.maximum(cells.astype(F32), 0.0)
            column = lax.broadcasted_iota(jnp.int32, cells.shape, 1)
            left = jnp.where(column == 0, 0.0, pltpu.roll(cells, 1, 1))
            right = jnp.where(column == columns - 1, 0.0, pltpu.roll(cells, columns - 1, 1))
            shifts[0, row, pl.ds(start, step), :] = left.astype(BF16)
            shifts[1, row, pl.ds(start, step), :] = cells.astype(BF16)
            shifts[2, row, pl.ds(start, step), :] = right.astype(BF16)


def shift(above, middle, below, name):
    tile_rows, channels, columns = middle.shape
    return pl.pallas_call(
        fill_shifts,
        out_shape=jax.ShapeDtypeStruct((3, tile_rows + 2, channels, columns), BF16),
        in_specs=[VMEM] * 3,
        out_specs=VMEM,
        compiler_params=params(32),
        cost_estimate=cost(10**7, 8 * tile_rows * channels * columns),
        name=name,
    )(above, middle, below)


def band_slice(band):
    return pl.ds(pl.multiple_of(band * LANES, LANES), LANES)


def unfolded(shifts, band, tile_rows):
    taps = []
    for shift_y in range(3):
        for shift_x in range(3):
            rows = [shifts[shift_x, shift_y + row, :, band_slice(band)] for row in range(tile_rows)]
            taps.append(jnp.concatenate(rows, axis=1))
    return jnp.concatenate(taps, axis=0)


def band_weights(pieces, groups, place_of, band):
    def rows_of(part, place, start, count):
        for piece in pieces:
            if start < piece.shape[2]:
                return piece.at[part, place][start : start + count, :]
            start -= piece.shape[2]

    wide, last = [], []
    tail = 64 * pairs_of(groups)
    for slot in range(2):
        place = place_of[2 * band + slot]
        blocks = [rows_of(part, place, start, 64) for part in range(groups) for start in range(0, tail, 64)]
        wide.append(jnp.concatenate(blocks, axis=1))
        rest = [rows_of(part, place, tail, tail_of(groups)) for part in range(groups)]
        rest = jnp.concatenate(rest, axis=0)
        last.extend([rest[:, :64], rest[:, 64:]])
    return jnp.concatenate(wide, axis=0), jnp.concatenate(last, axis=0)


def first_mask(regions, listed, band, channels, tile_rows):
    rows = [regions[row : row + 1, band_slice(band)] for row in range(tile_rows)]
    flat = jnp.concatenate(rows, axis=1)
    return jnp.broadcast_to(flat, (channels, flat.shape[1])) == listed[2 * band]


def masked(upstream, mask):
    wide = upstream.astype(F32)
    first = jnp.where(mask, wide, 0.0).astype(BF16)
    second = jnp.where(mask, 0.0, wide).astype(BF16)
    return jnp.concatenate([first, second], axis=0)


def side_by_side(cells, band, tile_rows):
    return jnp.concatenate([cells[row, :, band_slice(band)] for row in range(tile_rows)], axis=1)


def dot(left, right, left_dim, right_dim):
    return lax.dot_general(
        left, right, (((left_dim,), (right_dim,)), ((), ())), preferred_element_type=F32
    )


def conv_kernel(position, listed, regions, middle, shifts, *rest):
    pieces, out = rest[:-1], rest[-1]
    tile_rows, channels, columns = middle.shape

    @pl.loop(0, columns // LANES, unroll=4)
    def _(band):
        cells = unfolded(shifts, band, tile_rows)
        wide, last = band_weights(pieces, pieces[0].shape[0], position, band)
        both = dot(wide, cells[:512], 1, 0) + dot(last, cells[512:], 1, 0)
        mask = first_mask(regions, listed, band, channels, tile_rows)
        mixed = jnp.where(mask, both[:channels], both[channels:])
        for row in range(tile_rows):
            here = mixed[:, row * LANES : (row + 1) * LANES]
            here = here + middle[row, :, band_slice(band)].astype(F32)
            out[row, :, band_slice(band)] = here.astype(BF16)


def conv(position, listed, regions, middle, shifts, kernels, name, room=32):
    tile_rows, channels, columns = middle.shape
    return pl.pallas_call(
        conv_kernel,
        out_shape=jax.ShapeDtypeStruct(middle.shape, BF16),
        in_specs=[SMEM, SMEM] + [VMEM] * (3 + len(kernels)),
        out_specs=VMEM,
        compiler_params=params(room),
        cost_estimate=cost(4 * 9 * channels * channels * columns * tile_rows, 5000000),
        name=name,
    )(position, listed, regions, middle, shifts, *kernels)


def store_rows(out, band, cells):
    for row in range(out.shape[0]):
        out[row, :, band_slice(band)] = cells[:, row * LANES : (row + 1) * LANES]


def store_partial(groups, position, band, upstream, cells, mask, out):
    channels = upstream.shape[0]
    sums = dot(masked(upstream, mask), cells, 1, 1).astype(BF16)
    for slot in range(2):
        mine = sums[channels * slot : channels * (slot + 1)]
        there = out.at[position[2 * band + slot]]
        for pair in range(4):
            start = pair_start(pair, groups)
            there[start : start + 64, :] = mine[:, LANES * pair : LANES * (pair + 1)]
        rest = jnp.concatenate([mine[:32, 512:], mine[32:, 512:]], axis=1)
        size = tail_of(groups)
        for part in range(groups):
            start = tail_start(part, groups)
            there[start : start + size, :] = rest[size * part : size * (part + 1)]


def partial_kernel(groups, position, listed, regions, upstream, above, middle, below, out, shifts):
    tile_rows, channels, columns = upstream.shape
    fill_shifts(above, middle, below, shifts)

    @pl.loop(0, columns // LANES, unroll=4)
    def _(band):
        cells = unfolded(shifts, band, tile_rows)
        mask = first_mask(regions, listed, band, channels, tile_rows)
        store_partial(groups, position, band, side_by_side(upstream, band, tile_rows), cells, mask, out)


def partial_of(position, listed, regions, upstream, above, middle, below, places, groups):
    tile_rows, channels, columns = middle.shape
    rows = 9 * channels * channels // LANES
    return pl.pallas_call(
        functools.partial(partial_kernel, groups),
        out_shape=(
            jax.ShapeDtypeStruct((places, rows, LANES), BF16),
            jax.ShapeDtypeStruct((3, tile_rows + 2, channels, columns), BF16),
        ),
        in_specs=[SMEM, SMEM] + [VMEM] * 5,
        out_specs=(VMEM, VMEM),
        compiler_params=params(56),
        cost_estimate=cost(4 * 9 * channels * channels * columns * tile_rows, 8000000),
        name="partial_1",
    )(position, listed, regions, upstream, above, middle, below)


def carried_kernel(
    groups, position, listed, regions, cotangent, hidden, inner, from_above, from_below, shifts, carried, out
):
    tile_rows, channels, columns = hidden.shape

    @pl.loop(0, columns // LANES, unroll=4)
    def _(band):
        cells = unfolded(shifts, band, tile_rows)
        mask = first_mask(regions, listed, band, channels, tile_rows)
        back = []
        for row in range(tile_rows):
            value = inner[row, :, band_slice(band)]
            if row == 0:
                value = value + from_above[:, band_slice(band)].astype(F32)
            if row == tile_rows - 1:
                value = value + from_below[:, band_slice(band)].astype(F32)
            back.append(value)
        keep = side_by_side(hidden, band, tile_rows).astype(F32) > 0.0
        back = jnp.where(keep, jnp.concatenate(back, axis=1), 0.0)
        upstream = (side_by_side(cotangent, band, tile_rows).astype(F32) + back).astype(BF16)
        store_rows(carried, band, upstream)
        store_partial(groups, position, band, upstream, cells, mask, out)


def carried_of(
    position, listed, regions, cotangent, hidden, inner, from_above, from_below, shifts, places, groups
):
    tile_rows, channels, columns = hidden.shape
    rows = 9 * channels * channels // LANES
    return pl.pallas_call(
        functools.partial(carried_kernel, groups),
        out_shape=(
            jax.ShapeDtypeStruct(hidden.shape, BF16),
            jax.ShapeDtypeStruct((places, rows, LANES), BF16),
        ),
        in_specs=[SMEM, SMEM] + [VMEM] * 7,
        out_specs=(VMEM, VMEM),
        compiler_params=params(32),
        cost_estimate=cost(4 * 9 * channels * channels * columns * tile_rows, 7000000),
        name="carried_partial_0",
    )(position, listed, regions, cotangent, hidden, inner, from_above, from_below, shifts)


def spread_kernel(position, listed, regions, upstream, *rest):
    pieces, (inner, edges, total) = rest[:-3], rest[-3:]
    tile_rows, channels, columns = upstream.shape
    total[...] = jnp.zeros_like(total)

    @pl.loop(0, columns // LANES, unroll=4)
    def _(band):
        wide, last = band_weights(pieces, pieces[0].shape[0], position, band)
        mask = first_mask(regions, listed, band, channels, tile_rows)
        both = masked(side_by_side(upstream, band, tile_rows), mask)
        spread = jnp.concatenate([dot(wide, both, 0, 0), dot(last, both, 0, 0)], axis=0)
        lane = lax.broadcasted_iota(jnp.int32, (channels, LANES), 1)
        for target in range(tile_rows + 2):
            moved = []
            for shift_x in range(3):
                value = None
                for row in range(tile_rows):
                    shift_y = target - 1 - row + 1
                    if 0 <= shift_y <= 2:
                        tap = 3 * shift_y + shift_x
                        piece = spread[
                            channels * tap : channels * (tap + 1), LANES * row : LANES * (row + 1)
                        ]
                        value = piece if value is None else value + piece
                moved.append(value)
            left = pltpu.roll(moved[0], LANES - 1, 1)
            right = pltpu.roll(moved[2], 1, 1)
            centre = (
                moved[1]
                + jnp.where(lane == LANES - 1, 0.0, left)
                + jnp.where(lane == 0, 0.0, right)
            )
            total[target, :, band_slice(band)] += jnp.where(lane == LANES - 1, left, 0.0)
            total[target, :, band_slice(band + 1)] += centre
            total[target, :, band_slice(band + 2)] += jnp.where(lane == 0, right, 0.0)

    for row in range(tile_rows):
        inner[row] = total[row + 1, :, LANES : LANES + columns]
    edges[0] = total[0, :, LANES : LANES + columns].astype(BF16)
    edges[1] = total[tile_rows + 1, :, LANES : LANES + columns].astype(BF16)


def spread_of(position, listed, regions, upstream, kernels, name, room=32):
    tile_rows, channels, columns = upstream.shape
    return pl.pallas_call(
        spread_kernel,
        out_shape=(
            jax.ShapeDtypeStruct(upstream.shape, F32),
            jax.ShapeDtypeStruct((2, channels, columns), BF16),
        ),
        in_specs=[SMEM, SMEM] + [VMEM] * (2 + len(kernels)),
        out_specs=(VMEM, VMEM),
        scratch_shapes=[pltpu.VMEM((tile_rows + 2, channels, columns + 2 * LANES), F32)],
        compiler_params=params(room),
        cost_estimate=cost(4 * 9 * channels * channels * columns * tile_rows, 5000000),
        name=name,
    )(position, listed, regions, upstream, *kernels)


GY = ("far", "near")
PLANE = ("groups", "near")
ALL = ("groups", "far", "near")


def from_neighbours(upper, lower):
    count = lax.axis_size(GY)
    above = lax.ppermute(upper, GY, [(i, i + 1) for i in range(count - 1)])
    below = lax.ppermute(lower, GY, [(i + 1, i) for i in range(count - 1)])
    return above, below


def exchange(value, axes):
    return lax.all_to_all(value, axes, split_axis=0, concat_axis=0, tiled=True)


def after(first, value):
    return lax.optimization_barrier((*first, value))


def places_for(owner, owners, per_owner, content):
    order = jnp.arange(owner.shape[0], dtype=jnp.int32)
    earlier = (owner[:, None] == owner[None, :]) & (order[None, :] < order[:, None])
    position = owner * per_owner + jnp.sum(earlier.astype(jnp.int32), axis=-1)
    hits = position[None, :] == jnp.arange(owners * per_owner, dtype=jnp.int32)[:, None]
    wanted = jnp.max(jnp.where(hits, content[None, :], -1), axis=1)
    return position, wanted.reshape(owners, per_owner)


def body(field, cotangent, banks, region_map, tile_regions, bank_slot):
    col_bands = tile_regions.shape[0]
    groups, far, near = (lax.axis_size(axis) for axis in ALL)
    devices = far * near
    per_dev = banks.shape[1]
    slots_per = max(1, 2 * col_bands // devices)
    places = devices * slots_per
    listed = tile_regions.reshape(-1)
    bank_row = bank_slot[listed]
    holder = bank_row // per_dev
    local_row = bank_row % per_dev
    position, wanted = places_for(holder, devices, slots_per, local_row)
    my_group, my_far = lax.axis_index("groups"), lax.axis_index("far")

    cells = jnp.transpose(field, (1, 0, 2))
    upstream = jnp.transpose(cotangent, (1, 0, 2))
    last = cells.shape[0] - 1
    where = (position, listed, region_map)

    message = jnp.transpose(wanted.reshape(far, near, slots_per), (1, 0, 2))
    message = jnp.broadcast_to(message[None, None], (groups, far, near, far, slots_per))
    own_part = my_group.astype(jnp.int32).reshape(1)
    message = exchange(message.reshape(groups * devices, far * slots_per), ALL)
    message = message.reshape(groups, far, near, far, slots_per)
    mine = lax.dynamic_index_in_dim(message, my_group, 0, False)
    requested = lax.dynamic_index_in_dim(mine, my_far, 2, False).reshape(-1)
    asked = lax.dynamic_index_in_dim(message, my_far, 1, False).reshape(groups * near, far, slots_per)
    steps = jnp.arange(far, dtype=jnp.int32)
    asked = jnp.maximum(jnp.take(asked, (my_far - steps) % far, axis=1), 0)
    asked = asked.reshape(groups * near, far * slots_per)

    step = (my_far - holder // near) % far
    place = (holder % near * far + step) * slots_per + position % slots_per
    fetch = (place.astype(jnp.int32), listed, region_map)

    above, below = from_neighbours(cells[last], cells[0])
    turns = [[(k, (k + turn) % far) for k in range(far)] for turn in range(1, far)]
    whole = part_rows(groups)
    wire_a, wire_b = wire(own_part, banks, 1, groups, (64, whole - 64))
    (wire_zero,) = wire(own_part, banks, 0, groups, (whole,))

    def gathered(mine):
        return [mine] + [lax.ppermute(mine, "far", turn) for turn in turns]

    def fetched(buffers, name):
        arrived = exchange(pack(asked, buffers, name), PLANE)
        return arrived.reshape(groups, near * far * slots_per, *arrived.shape[1:])

    bank_a = gathered(wire_a)
    *bank_a, wire_b = after(bank_a, wire_b)
    bank_b = gathered(wire_b)
    *bank_b, above, below, wire_zero = after((*bank_b, above, below), wire_zero)
    bank_zero = gathered(wire_zero)
    kernel_one = [fetched(bank_a, "pack_1a"), fetched(bank_b, "pack_1b")]
    kernel_zero = [fetched(bank_zero, "pack_0")]
    shifts = shift(above, cells, below, "shift_0")
    shifts, upstream_one = after((shifts,), upstream)
    inner_one, edges_one = spread_of(*fetch, upstream_one, kernel_one, "spread_1")
    from_above, from_below = from_neighbours(edges_one[1], edges_one[0])
    hidden = conv(*fetch, cells, shifts, kernel_zero, "conv_0")
    hidden_above, hidden_below = from_neighbours(hidden[last], hidden[0])
    carried, partial_zero = carried_of(
        *where, upstream, hidden, inner_one, from_above, from_below, shifts, places, groups
    )
    hidden_above, hidden_below, partial_zero = after((hidden_above, hidden_below), partial_zero)
    around = (hidden_above, hidden, hidden_below)
    sent_zero = exchange(partial_zero, GY)
    inner_zero, edges_zero = spread_of(*fetch, carried, kernel_zero, "spread_0", 56)
    from_above, from_below = from_neighbours(edges_zero[1], edges_zero[0])
    partial_one, shifts_one = partial_of(*where, upstream, *around, places, groups)
    from_above, from_below, partial_one = after((from_above, from_below), partial_one)
    sent_one = exchange(partial_one, GY)
    refined = conv(*fetch, hidden, shifts_one, kernel_one, "conv_1", 56)
    back = inner_zero.at[0].add(from_above.astype(F32)).at[last].add(from_below.astype(F32))
    input_grad = (carried.astype(F32) + jnp.where(cells > 0, back, 0.0)).astype(BF16)
    half = total_of(requested, sent_zero, banks, 0, groups)
    grad_banks = total_of(requested, sent_one, banks, 1, groups, half)
    return (jnp.transpose(refined, (1, 0, 2)), jnp.transpose(input_grad, (1, 0, 2)), grad_banks)


def solution(mesh):
    groups, devices = mesh.shape["groups"], mesh.shape["gy"]
    cut = Mesh(mesh.devices.reshape(groups, devices // NEAR, NEAR), ALL)
    return jax.shard_map(
        body,
        mesh=cut,
        in_specs=(
            P(None, ALL, None),
            P(None, ALL, None),
            P(None, GY, None),
            P(ALL, None),
            P(ALL, None),
            P("groups"),
        ),
        out_specs=(
            P(None, ALL, None),
            P(None, ALL, None),
            P("groups", GY, None),
        ),
        check_vma=False,
    )
```

```python
import functools

import jax
import jax.numpy as jnp
from jax import lax
from jax.experimental import pallas as pl
from jax.experimental.pallas import tpu as pltpu
from jax.sharding import Mesh
from jax.sharding import PartitionSpec as P

grad_unscale = 0.03125
F32 = jnp.float32
BF16 = jnp.bfloat16
LANES = 128
VMEM = pl.BlockSpec(memory_space=pltpu.VMEM)
SMEM = pl.BlockSpec(memory_space=pltpu.SMEM)
HBM = pl.BlockSpec(memory_space=pl.ANY)

NEAR = 4


def pairs_of(parts):
    return 4 // parts


def tail_of(parts):
    return 32 // parts


def part_rows(parts):
    return 64 * pairs_of(parts) + tail_of(parts)


def pair_start(pair, parts):
    return pair // pairs_of(parts) * part_rows(parts) + 64 * (pair % pairs_of(parts))


def tail_start(part, parts):
    return part * part_rows(parts) + 64 * pairs_of(parts)


def params(mib):
    return pltpu.CompilerParams(vmem_limit_bytes=mib * 2**20)


def cost(flops, moved):
    return pl.CostEstimate(flops=flops, bytes_accessed=moved, transcendentals=0)


def swap_halves(tile):
    return pltpu.roll(tile, LANES // 2, 1)


def low_half(tile):
    return lax.broadcasted_iota(jnp.int32, tile.shape, 1) < LANES // 2


def wire_kernel(parts, per_dev, rows, own_part, banks, *rest):
    outs, (natural, travel) = rest[:-2], rest[-2:]
    for part in range(parts):

        @pl.when(own_part[0] == part)
        def _(part=part):
            pairs = range(part * pairs_of(parts), (part + 1) * pairs_of(parts))
            half = tail_of(parts) // 2
            for chunk in [*range(64 * pairs[0], 64 * pairs[-1] + 64), *range(256, rows)]:
                tile = banks[0, :, chunk * LANES : (chunk + 1) * LANES].astype(F32)
                natural[pl.ds(chunk, per_dev, stride=rows), :] = tile

            @pl.loop(0, per_dev)
            def _(row):
                base = row * rows

                def blend(first, second, start, count):
                    first = natural[pl.ds(base + first, count), :]
                    second = natural[pl.ds(base + second, count), :]
                    even = jnp.where(low_half(first), first, swap_halves(second))
                    odd = jnp.where(low_half(first), swap_halves(first), second)
                    travel[pl.ds(start, count, stride=2), :] = even
                    travel[pl.ds(start + 1, count, stride=2), :] = odd

                for order, pair in enumerate(pairs):
                    blend(64 * pair, 64 * pair + 32, 64 * order, 32)
                blend(256 + part * half, 272 + part * half, 64 * len(pairs), half)
                start = 0
                for out in outs:
                    out[row] = travel[start : start + out.shape[1], :].astype(BF16)
                    start += out.shape[1]


def wire(own_part, banks, layer, parts, sizes):
    layers, per_dev, width = banks.shape
    rows = width // LANES
    return pl.pallas_call(
        functools.partial(wire_kernel, parts, per_dev, rows),
        grid=(1,),
        out_shape=[jax.ShapeDtypeStruct((per_dev, size, LANES), BF16) for size in sizes],
        in_specs=[SMEM, pl.BlockSpec((1, per_dev, width), lambda step: (layer, 0, 0))],
        out_specs=[pl.BlockSpec((per_dev, size, LANES), lambda step: (0, 0, 0)) for size in sizes],
        scratch_shapes=[
            pltpu.VMEM((per_dev * rows, LANES), F32),
            pltpu.VMEM((part_rows(parts), LANES), F32),
        ],
        compiler_params=params(24),
        cost_estimate=cost(10**6, 4 * per_dev * width),
        name=f"wire_{layer}",
    )(own_part, banks)


def pack_kernel(rows, *refs):
    buffers, out = refs[:-1], refs[-1]
    inner = rows.shape[1]
    slots = inner // len(buffers)

    @pl.loop(0, rows.shape[0])
    def _(target):
        for entry in range(inner):
            out[target * inner + entry] = buffers[entry // slots][rows[target, entry]]


def pack(rows, buffers, name):
    targets, inner = rows.shape
    shape = buffers[0].shape[1:]
    return pl.pallas_call(
        pack_kernel,
        out_shape=jax.ShapeDtypeStruct((targets * inner, *shape), BF16),
        in_specs=[SMEM] + [VMEM] * len(buffers),
        out_specs=VMEM,
        compiler_params=params(32),
        cost_estimate=cost(10**11, 4 * targets * inner * shape[0] * shape[1]),
        name=name,
    )(rows, *buffers)


def total_kernel(groups, per_dev, rows, requested, parts, *rest):
    out, total, natural = rest[-3:]
    total[...] = jnp.zeros_like(total)

    @pl.loop(0, parts.shape[0], unroll=4)
    def _(place):
        row = jnp.where(requested[place] < 0, per_dev, requested[place])
        total[pl.ds(pl.multiple_of(row * rows, 8), rows), :] += parts[place].astype(F32)

    @pl.loop(0, per_dev, unroll=2)
    def _(row):
        base = row * rows

        def split(start, count, first, second):
            even = total[pl.ds(base + start, count, stride=2), :] * grad_unscale
            odd = total[pl.ds(base + start + 1, count, stride=2), :] * grad_unscale
            natural[pl.ds(base + first, count), :] = jnp.where(low_half(even), even, swap_halves(odd))
            natural[pl.ds(base + second, count), :] = jnp.where(low_half(even), swap_halves(even), odd)

        for pair in range(4):
            split(pair_start(pair, groups), 32, 64 * pair, 64 * pair + 32)
        half = tail_of(groups) // 2
        for part in range(groups):
            split(tail_start(part, groups), half, 256 + part * half, 272 + part * half)

    for chunk in range(rows):
        out[0, :, chunk * LANES : (chunk + 1) * LANES] = natural[pl.ds(chunk, per_dev, stride=rows), :]


def total_of(requested, parts, banks, layer, groups, earlier=None):
    layers, per_dev, width = banks.shape
    rows = width // LANES
    places = requested.shape[0]
    args, specs = [requested, parts], [SMEM, pl.BlockSpec(parts.shape, lambda step: (0, 0, 0))]
    if earlier is not None:
        args.append(earlier)
        specs.append(HBM)
    return pl.pallas_call(
        functools.partial(total_kernel, groups, per_dev, rows),
        grid=(1,),
        out_shape=jax.ShapeDtypeStruct((layers, per_dev, width), F32),
        in_specs=specs,
        out_specs=pl.BlockSpec((1, per_dev, width), lambda step: (layer, 0, 0)),
        scratch_shapes=[
            pltpu.VMEM(((per_dev + 1) * rows, LANES), F32),
            pltpu.VMEM((per_dev * rows, LANES), F32),
        ],
        input_output_aliases={2: 0} if earlier is not None else {},
        compiler_params=params(32),
        cost_estimate=cost(1000000, 2 * places * width + 4 * per_dev * width),
        name=f"total_{layer}",
    )(*args)


def fill_shifts(above, middle, below, shifts):
    tile_rows, channels, columns = middle.shape
    step = 16

    @pl.loop(0, channels // step)
    def _(group):
        start = pl.multiple_of(group * step, step)
        for row in range(tile_rows + 2):
            if row == 0:
                cells = above[pl.ds(start, step), :]
            elif row == tile_rows + 1:
                cells = below[pl.ds(start, step), :]
            else:
                cells = middle[row - 1, pl.ds(start, step), :]
            cells = jnp.maximum(cells.astype(F32), 0.0)
            column = lax.broadcasted_iota(jnp.int32, cells.shape, 1)
            left = jnp.where(column == 0, 0.0, pltpu.roll(cells, 1, 1))
            right = jnp.where(column == columns - 1, 0.0, pltpu.roll(cells, columns - 1, 1))
            shifts[0, row, pl.ds(start, step), :] = left.astype(BF16)
            shifts[1, row, pl.ds(start, step), :] = cells.astype(BF16)
            shifts[2, row, pl.ds(start, step), :] = right.astype(BF16)


def shift(above, middle, below, name):
    tile_rows, channels, columns = middle.shape
    return pl.pallas_call(
        fill_shifts,
        out_shape=jax.ShapeDtypeStruct((3, tile_rows + 2, channels, columns), BF16),
        in_specs=[VMEM] * 3,
        out_specs=VMEM,
        compiler_params=params(32),
        cost_estimate=cost(10**7, 8 * tile_rows * channels * columns),
        name=name,
    )(above, middle, below)


def band_slice(band):
    return pl.ds(pl.multiple_of(band * LANES, LANES), LANES)


def unfolded(shifts, band, tile_rows):
    taps = []
    for shift_y in range(3):
        for shift_x in range(3):
            rows = [shifts[shift_x, shift_y + row, :, band_slice(band)] for row in range(tile_rows)]
            taps.append(jnp.concatenate(rows, axis=1))
    return jnp.concatenate(taps, axis=0)


def band_weights(pieces, groups, place_of, band):
    def rows_of(part, place, start, count):
        for piece in pieces:
            if start < piece.shape[2]:
                return piece.at[part, place][start : start + count, :]
            start -= piece.shape[2]

    wide, last = [], []
    tail = 64 * pairs_of(groups)
    for slot in range(2):
        place = place_of[2 * band + slot]
        blocks = [rows_of(part, place, start, 64) for part in range(groups) for start in range(0, tail, 64)]
        wide.append(jnp.concatenate(blocks, axis=1))
        rest = [rows_of(part, place, tail, tail_of(groups)) for part in range(groups)]
        rest = jnp.concatenate(rest, axis=0)
        last.extend([rest[:, :64], rest[:, 64:]])
    return jnp.concatenate(wide, axis=0), jnp.concatenate(last, axis=0)


def first_mask(regions, listed, band, channels, tile_rows):
    rows = [regions[row : row + 1, band_slice(band)] for row in range(tile_rows)]
    flat = jnp.concatenate(rows, axis=1)
    return jnp.broadcast_to(flat, (channels, flat.shape[1])) == listed[2 * band]


def masked(upstream, mask):
    wide = upstream.astype(F32)
    first = jnp.where(mask, wide, 0.0).astype(BF16)
    second = jnp.where(mask, 0.0, wide).astype(BF16)
    return jnp.concatenate([first, second], axis=0)


def side_by_side(cells, band, tile_rows):
    return jnp.concatenate([cells[row, :, band_slice(band)] for row in range(tile_rows)], axis=1)


def dot(left, right, left_dim, right_dim):
    return lax.dot_general(
        left, right, (((left_dim,), (right_dim,)), ((), ())), preferred_element_type=F32
    )


def conv_kernel(position, listed, regions, middle, shifts, *rest):
    pieces, out = rest[:-1], rest[-1]
    tile_rows, channels, columns = middle.shape

    @pl.loop(0, columns // LANES, unroll=4)
    def _(band):
        cells = unfolded(shifts, band, tile_rows)
        wide, last = band_weights(pieces, pieces[0].shape[0], position, band)
        both = dot(wide, cells[:512], 1, 0) + dot(last, cells[512:], 1, 0)
        mask = first_mask(regions, listed, band, channels, tile_rows)
        mixed = jnp.where(mask, both[:channels], both[channels:])
        for row in range(tile_rows):
            here = mixed[:, row * LANES : (row + 1) * LANES]
            here = here + middle[row, :, band_slice(band)].astype(F32)
            out[row, :, band_slice(band)] = here.astype(BF16)


def conv(position, listed, regions, middle, shifts, kernels, name, room=32):
    tile_rows, channels, columns = middle.shape
    return pl.pallas_call(
        conv_kernel,
        out_shape=jax.ShapeDtypeStruct(middle.shape, BF16),
        in_specs=[SMEM, SMEM] + [VMEM] * (3 + len(kernels)),
        out_specs=VMEM,
        compiler_params=params(room),
        cost_estimate=cost(4 * 9 * channels * channels * columns * tile_rows, 5000000),
        name=name,
    )(position, listed, regions, middle, shifts, *kernels)


def store_rows(out, band, cells):
    for row in range(out.shape[0]):
        out[row, :, band_slice(band)] = cells[:, row * LANES : (row + 1) * LANES]


def store_partial(groups, position, band, upstream, cells, mask, out):
    channels = upstream.shape[0]
    sums = dot(masked(upstream, mask), cells, 1, 1).astype(BF16)
    for slot in range(2):
        mine = sums[channels * slot : channels * (slot + 1)]
        there = out.at[position[2 * band + slot]]
        for pair in range(4):
            start = pair_start(pair, groups)
            there[start : start + 64, :] = mine[:, LANES * pair : LANES * (pair + 1)]
        rest = jnp.concatenate([mine[:32, 512:], mine[32:, 512:]], axis=1)
        size = tail_of(groups)
        for part in range(groups):
            start = tail_start(part, groups)
            there[start : start + size, :] = rest[size * part : size * (part + 1)]


def partial_kernel(groups, position, listed, regions, upstream, above, middle, below, out, shifts):
    tile_rows, channels, columns = upstream.shape
    fill_shifts(above, middle, below, shifts)

    @pl.loop(0, columns // LANES, unroll=4)
    def _(band):
        cells = unfolded(shifts, band, tile_rows)
        mask = first_mask(regions, listed, band, channels, tile_rows)
        store_partial(groups, position, band, side_by_side(upstream, band, tile_rows), cells, mask, out)


def partial_of(position, listed, regions, upstream, above, middle, below, places, groups):
    tile_rows, channels, columns = middle.shape
    rows = 9 * channels * channels // LANES
    return pl.pallas_call(
        functools.partial(partial_kernel, groups),
        out_shape=(
            jax.ShapeDtypeStruct((places, rows, LANES), BF16),
            jax.ShapeDtypeStruct((3, tile_rows + 2, channels, columns), BF16),
        ),
        in_specs=[SMEM, SMEM] + [VMEM] * 5,
        out_specs=(VMEM, VMEM),
        compiler_params=params(56),
        cost_estimate=cost(4 * 9 * channels * channels * columns * tile_rows, 8000000),
        name="partial_1",
    )(position, listed, regions, upstream, above, middle, below)


def carried_kernel(
    groups, position, listed, regions, cotangent, hidden, inner, from_above, from_below, shifts, carried, out
):
    tile_rows, channels, columns = hidden.shape

    @pl.loop(0, columns // LANES, unroll=4)
    def _(band):
        cells = unfolded(shifts, band, tile_rows)
        mask = first_mask(regions, listed, band, channels, tile_rows)
        back = []
        for row in range(tile_rows):
            value = inner[row, :, band_slice(band)]
            if row == 0:
                value = value + from_above[:, band_slice(band)].astype(F32)
            if row == tile_rows - 1:
                value = value + from_below[:, band_slice(band)].astype(F32)
            back.append(value)
        keep = side_by_side(hidden, band, tile_rows).astype(F32) > 0.0
        back = jnp.where(keep, jnp.concatenate(back, axis=1), 0.0)
        upstream = (side_by_side(cotangent, band, tile_rows).astype(F32) + back).astype(BF16)
        store_rows(carried, band, upstream)
        store_partial(groups, position, band, upstream, cells, mask, out)


def carried_of(
    position, listed, regions, cotangent, hidden, inner, from_above, from_below, shifts, places, groups
):
    tile_rows, channels, columns = hidden.shape
    rows = 9 * channels * channels // LANES
    return pl.pallas_call(
        functools.partial(carried_kernel, groups),
        out_shape=(
            jax.ShapeDtypeStruct(hidden.shape, BF16),
            jax.ShapeDtypeStruct((places, rows, LANES), BF16),
        ),
        in_specs=[SMEM, SMEM] + [VMEM] * 7,
        out_specs=(VMEM, VMEM),
        compiler_params=params(32),
        cost_estimate=cost(4 * 9 * channels * channels * columns * tile_rows, 7000000),
        name="carried_partial_0",
    )(position, listed, regions, cotangent, hidden, inner, from_above, from_below, shifts)


def spread_kernel(position, listed, regions, upstream, *rest):
    pieces, (inner, edges, total) = rest[:-3], rest[-3:]
    tile_rows, channels, columns = upstream.shape
    total[...] = jnp.zeros_like(total)

    @pl.loop(0, columns // LANES, unroll=4)
    def _(band):
        wide, last = band_weights(pieces, pieces[0].shape[0], position, band)
        mask = first_mask(regions, listed, band, channels, tile_rows)
        both = masked(side_by_side(upstream, band, tile_rows), mask)
        spread = jnp.concatenate([dot(wide, both, 0, 0), dot(last, both, 0, 0)], axis=0)
        lane = lax.broadcasted_iota(jnp.int32, (channels, LANES), 1)
        for target in range(tile_rows + 2):
            moved = []
            for shift_x in range(3):
                value = None
                for row in range(tile_rows):
                    shift_y = target - 1 - row + 1
                    if 0 <= shift_y <= 2:
                        tap = 3 * shift_y + shift_x
                        piece = spread[
                            channels * tap : channels * (tap + 1), LANES * row : LANES * (row + 1)
                        ]
                        value = piece if value is None else value + piece
                moved.append(value)
            left = pltpu.roll(moved[0], LANES - 1, 1)
            right = pltpu.roll(moved[2], 1, 1)
            centre = (
                moved[1]
                + jnp.where(lane == LANES - 1, 0.0, left)
                + jnp.where(lane == 0, 0.0, right)
            )
            total[target, :, band_slice(band)] += jnp.where(lane == LANES - 1, left, 0.0)
            total[target, :, band_slice(band + 1)] += centre
            total[target, :, band_slice(band + 2)] += jnp.where(lane == 0, right, 0.0)

    for row in range(tile_rows):
        inner[row] = total[row + 1, :, LANES : LANES + columns]
    edges[0] = total[0, :, LANES : LANES + columns].astype(BF16)
    edges[1] = total[tile_rows + 1, :, LANES : LANES + columns].astype(BF16)


def spread_of(position, listed, regions, upstream, kernels, name, room=32):
    tile_rows, channels, columns = upstream.shape
    return pl.pallas_call(
        spread_kernel,
        out_shape=(
            jax.ShapeDtypeStruct(upstream.shape, F32),
            jax.ShapeDtypeStruct((2, channels, columns), BF16),
        ),
        in_specs=[SMEM, SMEM] + [VMEM] * (2 + len(kernels)),
        out_specs=(VMEM, VMEM),
        scratch_shapes=[pltpu.VMEM((tile_rows + 2, channels, columns + 2 * LANES), F32)],
        compiler_params=params(room),
        cost_estimate=cost(4 * 9 * channels * channels * columns * tile_rows, 5000000),
        name=name,
    )(position, listed, regions, upstream, *kernels)


GY = ("far", "near")
PLANE = ("groups", "near")
ALL = ("groups", "far", "near")


def from_neighbours(upper, lower):
    count = lax.axis_size(GY)
    above = lax.ppermute(upper, GY, [(i, i + 1) for i in range(count - 1)])
    below = lax.ppermute(lower, GY, [(i + 1, i) for i in range(count - 1)])
    return above, below


def exchange(value, axes):
    return lax.all_to_all(value, axes, split_axis=0, concat_axis=0, tiled=True)


def after(first, value):
    return lax.optimization_barrier((*first, value))


def places_for(owner, owners, per_owner, content):
    order = jnp.arange(owner.shape[0], dtype=jnp.int32)
    earlier = (owner[:, None] == owner[None, :]) & (order[None, :] < order[:, None])
    position = owner * per_owner + jnp.sum(earlier.astype(jnp.int32), axis=-1)
    hits = position[None, :] == jnp.arange(owners * per_owner, dtype=jnp.int32)[:, None]
    wanted = jnp.max(jnp.where(hits, content[None, :], -1), axis=1)
    return position, wanted.reshape(owners, per_owner)


def body(field, cotangent, banks, region_map, tile_regions, bank_slot):
    col_bands = tile_regions.shape[0]
    groups, far, near = (lax.axis_size(axis) for axis in ALL)
    devices = far * near
    per_dev = banks.shape[1]
    slots_per = max(1, 2 * col_bands // devices)
    places = devices * slots_per
    listed = tile_regions.reshape(-1)
    bank_row = bank_slot[listed]
    holder = bank_row // per_dev
    local_row = bank_row % per_dev
    position, wanted = places_for(holder, devices, slots_per, local_row)
    my_group, my_far = lax.axis_index("groups"), lax.axis_index("far")

    cells = jnp.transpose(field, (1, 0, 2))
    upstream = jnp.transpose(cotangent, (1, 0, 2))
    last = cells.shape[0] - 1
    where = (position, listed, region_map)

    message = jnp.transpose(wanted.reshape(far, near, slots_per), (1, 0, 2))
    message = jnp.broadcast_to(message[None, None], (groups, far, near, far, slots_per))
    own_part = my_group.astype(jnp.int32).reshape(1)
    message = exchange(message.reshape(groups * devices, far * slots_per), ALL)
    message = message.reshape(groups, far, near, far, slots_per)
    mine = lax.dynamic_index_in_dim(message, my_group, 0, False)
    requested = lax.dynamic_index_in_dim(mine, my_far, 2, False).reshape(-1)
    asked = lax.dynamic_index_in_dim(message, my_far, 1, False).reshape(groups * near, far, slots_per)
    steps = jnp.arange(far, dtype=jnp.int32)
    asked = jnp.maximum(jnp.take(asked, (my_far - steps) % far, axis=1), 0)
    asked = asked.reshape(groups * near, far * slots_per)

    step = (my_far - holder // near) % far
    place = (holder % near * far + step) * slots_per + position % slots_per
    fetch = (place.astype(jnp.int32), listed, region_map)

    above, below = from_neighbours(cells[last], cells[0])
    turns = [[(k, (k + turn) % far) for k in range(far)] for turn in range(1, far)]
    whole = part_rows(groups)
    wire_a, wire_b = wire(own_part, banks, 1, groups, (64, whole - 64))
    (wire_zero,) = wire(own_part, banks, 0, groups, (whole,))

    def gathered(mine):
        return [mine] + [lax.ppermute(mine, "far", turn) for turn in turns]

    def fetched(buffers, name):
        arrived = exchange(pack(asked, buffers, name), PLANE)
        return arrived.reshape(groups, near * far * slots_per, *arrived.shape[1:])

    bank_a = gathered(wire_a)
    *bank_a, wire_b = after(bank_a, wire_b)
    bank_b = gathered(wire_b)
    bank_b[-1], above, below, wire_zero = after((bank_b[-1], above, below), wire_zero)
    bank_zero = gathered(wire_zero)
    kernel_one = [fetched(bank_a, "pack_1a"), fetched(bank_b, "pack_1b")]
    kernel_zero = [fetched(bank_zero, "pack_0")]
    shifts = shift(above, cells, below, "shift_0")
    shifts, upstream_one = after((shifts,), upstream)
    inner_one, edges_one = spread_of(*fetch, upstream_one, kernel_one, "spread_1")
    from_above, from_below = from_neighbours(edges_one[1], edges_one[0])
    hidden = conv(*fetch, cells, shifts, kernel_zero, "conv_0")
    hidden_above, hidden_below = from_neighbours(hidden[last], hidden[0])
    carried, partial_zero = carried_of(
        *where, upstream, hidden, inner_one, from_above, from_below, shifts, places, groups
    )
    hidden_above, hidden_below, partial_zero = after((hidden_above, hidden_below), partial_zero)
    around = (hidden_above, hidden, hidden_below)
    sent_zero = exchange(partial_zero, GY)
    inner_zero, edges_zero = spread_of(*fetch, carried, kernel_zero, "spread_0", 56)
    from_above, from_below = from_neighbours(edges_zero[1], edges_zero[0])
    partial_one, shifts_one = partial_of(*where, upstream, *around, places, groups)
    from_above, from_below, partial_one = after((from_above, from_below), partial_one)
    sent_one = exchange(partial_one, GY)
    refined = conv(*fetch, hidden, shifts_one, kernel_one, "conv_1", 56)
    back = inner_zero.at[0].add(from_above.astype(F32)).at[last].add(from_below.astype(F32))
    input_grad = (carried.astype(F32) + jnp.where(cells > 0, back, 0.0)).astype(BF16)
    half = total_of(requested, sent_zero, banks, 0, groups)
    grad_banks = total_of(requested, sent_one, banks, 1, groups, half)
    return (jnp.transpose(refined, (1, 0, 2)), jnp.transpose(input_grad, (1, 0, 2)), grad_banks)


def solution(mesh):
    groups, devices = mesh.shape["groups"], mesh.shape["gy"]
    cut = Mesh(mesh.devices.reshape(groups, devices // NEAR, NEAR), ALL)
    return jax.shard_map(
        body,
        mesh=cut,
        in_specs=(
            P(None, ALL, None),
            P(None, ALL, None),
            P(None, GY, None),
            P(ALL, None),
            P(ALL, None),
            P("groups"),
        ),
        out_specs=(
            P(None, ALL, None),
            P(None, ALL, None),
            P("groups", GY, None),
        ),
        check_vma=False,
    )
```

```python
import functools

import jax
import jax.numpy as jnp
from jax import lax
from jax.experimental import pallas as pl
from jax.experimental.pallas import tpu as pltpu
from jax.sharding import Mesh
from jax.sharding import PartitionSpec as P

grad_unscale = 0.03125
F32 = jnp.float32
BF16 = jnp.bfloat16
LANES = 128
VMEM = pl.BlockSpec(memory_space=pltpu.VMEM)
SMEM = pl.BlockSpec(memory_space=pltpu.SMEM)
HBM = pl.BlockSpec(memory_space=pl.ANY)

NEAR = 4


def pairs_of(parts):
    return 4 // parts


def tail_of(parts):
    return 32 // parts


def part_rows(parts):
    return 64 * pairs_of(parts) + tail_of(parts)


def pair_start(pair, parts):
    return pair // pairs_of(parts) * part_rows(parts) + 64 * (pair % pairs_of(parts))


def tail_start(part, parts):
    return part * part_rows(parts) + 64 * pairs_of(parts)


def params(mib):
    return pltpu.CompilerParams(vmem_limit_bytes=mib * 2**20)


def cost(flops, moved):
    return pl.CostEstimate(flops=flops, bytes_accessed=moved, transcendentals=0)


def swap_halves(tile):
    return pltpu.roll(tile, LANES // 2, 1)


def low_half(tile):
    return lax.broadcasted_iota(jnp.int32, tile.shape, 1) < LANES // 2


def wire_kernel(parts, per_dev, rows, own_part, banks, *rest):
    outs, (natural, travel) = rest[:-2], rest[-2:]
    for part in range(parts):

        @pl.when(own_part[0] == part)
        def _(part=part):
            pairs = range(part * pairs_of(parts), (part + 1) * pairs_of(parts))
            half = tail_of(parts) // 2
            for chunk in [*range(64 * pairs[0], 64 * pairs[-1] + 64), *range(256, rows)]:
                tile = banks[0, :, chunk * LANES : (chunk + 1) * LANES].astype(F32)
                natural[pl.ds(chunk, per_dev, stride=rows), :] = tile

            @pl.loop(0, per_dev)
            def _(row):
                base = row * rows

                def blend(first, second, start, count):
                    first = natural[pl.ds(base + first, count), :]
                    second = natural[pl.ds(base + second, count), :]
                    even = jnp.where(low_half(first), first, swap_halves(second))
                    odd = jnp.where(low_half(first), swap_halves(first), second)
                    travel[pl.ds(start, count, stride=2), :] = even
                    travel[pl.ds(start + 1, count, stride=2), :] = odd

                for order, pair in enumerate(pairs):
                    blend(64 * pair, 64 * pair + 32, 64 * order, 32)
                blend(256 + part * half, 272 + part * half, 64 * len(pairs), half)
                start = 0
                for out in outs:
                    out[row] = travel[start : start + out.shape[1], :].astype(BF16)
                    start += out.shape[1]


def wire(own_part, banks, layer, parts, sizes):
    layers, per_dev, width = banks.shape
    rows = width // LANES
    return pl.pallas_call(
        functools.partial(wire_kernel, parts, per_dev, rows),
        grid=(1,),
        out_shape=[jax.ShapeDtypeStruct((per_dev, size, LANES), BF16) for size in sizes],
        in_specs=[SMEM, pl.BlockSpec((1, per_dev, width), lambda step: (layer, 0, 0))],
        out_specs=[pl.BlockSpec((per_dev, size, LANES), lambda step: (0, 0, 0)) for size in sizes],
        scratch_shapes=[
            pltpu.VMEM((per_dev * rows, LANES), F32),
            pltpu.VMEM((part_rows(parts), LANES), F32),
        ],
        compiler_params=params(24),
        cost_estimate=cost(10**6, 4 * per_dev * width),
        name=f"wire_{layer}",
    )(own_part, banks)


def pack_kernel(rows, *refs):
    buffers, out = refs[:-1], refs[-1]
    inner = rows.shape[1]
    slots = inner // len(buffers)

    @pl.loop(0, rows.shape[0])
    def _(target):
        for entry in range(inner):
            out[target * inner + entry] = buffers[entry // slots][rows[target, entry]]


def pack(rows, buffers, name):
    targets, inner = rows.shape
    shape = buffers[0].shape[1:]
    return pl.pallas_call(
        pack_kernel,
        out_shape=jax.ShapeDtypeStruct((targets * inner, *shape), BF16),
        in_specs=[SMEM] + [VMEM] * len(buffers),
        out_specs=VMEM,
        compiler_params=params(32),
        cost_estimate=cost(10**11, 4 * targets * inner * shape[0] * shape[1]),
        name=name,
    )(rows, *buffers)


def total_kernel(groups, per_dev, rows, requested, parts, *rest):
    out, total, natural = rest[-3:]
    total[...] = jnp.zeros_like(total)

    @pl.loop(0, parts.shape[0], unroll=8)
    def _(place):
        row = jnp.where(requested[place] < 0, per_dev, requested[place])
        total[pl.ds(pl.multiple_of(row * rows, 8), rows), :] += parts[place].astype(F32)

    @pl.loop(0, per_dev, unroll=2)
    def _(row):
        base = row * rows

        def split(start, count, first, second):
            even = total[pl.ds(base + start, count, stride=2), :] * grad_unscale
            odd = total[pl.ds(base + start + 1, count, stride=2), :] * grad_unscale
            natural[pl.ds(base + first, count), :] = jnp.where(low_half(even), even, swap_halves(odd))
            natural[pl.ds(base + second, count), :] = jnp.where(low_half(even), swap_halves(even), odd)

        for pair in range(4):
            split(pair_start(pair, groups), 32, 64 * pair, 64 * pair + 32)
        half = tail_of(groups) // 2
        for part in range(groups):
            split(tail_start(part, groups), half, 256 + part * half, 272 + part * half)

    for chunk in range(rows):
        out[0, :, chunk * LANES : (chunk + 1) * LANES] = natural[pl.ds(chunk, per_dev, stride=rows), :]


def total_of(requested, parts, banks, layer, groups, earlier=None):
    layers, per_dev, width = banks.shape
    rows = width // LANES
    places = requested.shape[0]
    args, specs = [requested, parts], [SMEM, pl.BlockSpec(parts.shape, lambda step: (0, 0, 0))]
    if earlier is not None:
        args.append(earlier)
        specs.append(HBM)
    return pl.pallas_call(
        functools.partial(total_kernel, groups, per_dev, rows),
        grid=(1,),
        out_shape=jax.ShapeDtypeStruct((layers, per_dev, width), F32),
        in_specs=specs,
        out_specs=pl.BlockSpec((1, per_dev, width), lambda step: (layer, 0, 0)),
        scratch_shapes=[
            pltpu.VMEM(((per_dev + 1) * rows, LANES), F32),
            pltpu.VMEM((per_dev * rows, LANES), F32),
        ],
        input_output_aliases={2: 0} if earlier is not None else {},
        compiler_params=params(32),
        cost_estimate=cost(1000000, 2 * places * width + 4 * per_dev * width),
        name=f"total_{layer}",
    )(*args)


def fill_shifts(above, middle, below, shifts):
    tile_rows, channels, columns = middle.shape
    step = 16

    @pl.loop(0, channels // step)
    def _(group):
        start = pl.multiple_of(group * step, step)
        for row in range(tile_rows + 2):
            if row == 0:
                cells = above[pl.ds(start, step), :]
            elif row == tile_rows + 1:
                cells = below[pl.ds(start, step), :]
            else:
                cells = middle[row - 1, pl.ds(start, step), :]
            cells = jnp.maximum(cells.astype(F32), 0.0)
            column = lax.broadcasted_iota(jnp.int32, cells.shape, 1)
            left = jnp.where(column == 0, 0.0, pltpu.roll(cells, 1, 1))
            right = jnp.where(column == columns - 1, 0.0, pltpu.roll(cells, columns - 1, 1))
            shifts[0, row, pl.ds(start, step), :] = left.astype(BF16)
            shifts[1, row, pl.ds(start, step), :] = cells.astype(BF16)
            shifts[2, row, pl.ds(start, step), :] = right.astype(BF16)


def shift(above, middle, below, name):
    tile_rows, channels, columns = middle.shape
    return pl.pallas_call(
        fill_shifts,
        out_shape=jax.ShapeDtypeStruct((3, tile_rows + 2, channels, columns), BF16),
        in_specs=[VMEM] * 3,
        out_specs=VMEM,
        compiler_params=params(32),
        cost_estimate=cost(10**7, 8 * tile_rows * channels * columns),
        name=name,
    )(above, middle, below)


def band_slice(band):
    return pl.ds(pl.multiple_of(band * LANES, LANES), LANES)


def unfolded(shifts, band, tile_rows):
    taps = []
    for shift_y in range(3):
        for shift_x in range(3):
            rows = [shifts[shift_x, shift_y + row, :, band_slice(band)] for row in range(tile_rows)]
            taps.append(jnp.concatenate(rows, axis=1))
    return jnp.concatenate(taps, axis=0)


def band_weights(pieces, groups, place_of, band):
    def rows_of(part, place, start, count):
        for piece in pieces:
            if start < piece.shape[2]:
                return piece.at[part, place][start : start + count, :]
            start -= piece.shape[2]

    wide, last = [], []
    tail = 64 * pairs_of(groups)
    for slot in range(2):
        place = place_of[2 * band + slot]
        blocks = [rows_of(part, place, start, 64) for part in range(groups) for start in range(0, tail, 64)]
        wide.append(jnp.concatenate(blocks, axis=1))
        rest = [rows_of(part, place, tail, tail_of(groups)) for part in range(groups)]
        rest = jnp.concatenate(rest, axis=0)
        last.extend([rest[:, :64], rest[:, 64:]])
    return jnp.concatenate(wide, axis=0), jnp.concatenate(last, axis=0)


def first_mask(regions, listed, band, channels, tile_rows):
    rows = [regions[row : row + 1, band_slice(band)] for row in range(tile_rows)]
    flat = jnp.concatenate(rows, axis=1)
    return jnp.broadcast_to(flat, (channels, flat.shape[1])) == listed[2 * band]


def masked(upstream, mask):
    wide = upstream.astype(F32)
    first = jnp.where(mask, wide, 0.0).astype(BF16)
    second = jnp.where(mask, 0.0, wide).astype(BF16)
    return jnp.concatenate([first, second], axis=0)


def side_by_side(cells, band, tile_rows):
    return jnp.concatenate([cells[row, :, band_slice(band)] for row in range(tile_rows)], axis=1)


def dot(left, right, left_dim, right_dim):
    return lax.dot_general(
        left, right, (((left_dim,), (right_dim,)), ((), ())), preferred_element_type=F32
    )


def conv_kernel(position, listed, regions, middle, shifts, *rest):
    pieces, out = rest[:-1], rest[-1]
    tile_rows, channels, columns = middle.shape

    @pl.loop(0, columns // LANES, unroll=8)
    def _(band):
        cells = unfolded(shifts, band, tile_rows)
        wide, last = band_weights(pieces, pieces[0].shape[0], position, band)
        both = dot(wide, cells[:512], 1, 0) + dot(last, cells[512:], 1, 0)
        mask = first_mask(regions, listed, band, channels, tile_rows)
        mixed = jnp.where(mask, both[:channels], both[channels:])
        for row in range(tile_rows):
            here = mixed[:, row * LANES : (row + 1) * LANES]
            here = here + middle[row, :, band_slice(band)].astype(F32)
            out[row, :, band_slice(band)] = here.astype(BF16)


def conv(position, listed, regions, middle, shifts, kernels, name, room=32):
    tile_rows, channels, columns = middle.shape
    return pl.pallas_call(
        conv_kernel,
        out_shape=jax.ShapeDtypeStruct(middle.shape, BF16),
        in_specs=[SMEM, SMEM] + [VMEM] * (3 + len(kernels)),
        out_specs=VMEM,
        compiler_params=params(room),
        cost_estimate=cost(4 * 9 * channels * channels * columns * tile_rows, 5000000),
        name=name,
    )(position, listed, regions, middle, shifts, *kernels)


def store_rows(out, band, cells):
    for row in range(out.shape[0]):
        out[row, :, band_slice(band)] = cells[:, row * LANES : (row + 1) * LANES]


def store_partial(groups, position, band, upstream, cells, mask, out):
    channels = upstream.shape[0]
    sums = dot(masked(upstream, mask), cells, 1, 1).astype(BF16)
    for slot in range(2):
        mine = sums[channels * slot : channels * (slot + 1)]
        there = out.at[position[2 * band + slot]]
        for pair in range(4):
            start = pair_start(pair, groups)
            there[start : start + 64, :] = mine[:, LANES * pair : LANES * (pair + 1)]
        rest = jnp.concatenate([mine[:32, 512:], mine[32:, 512:]], axis=1)
        size = tail_of(groups)
        for part in range(groups):
            start = tail_start(part, groups)
            there[start : start + size, :] = rest[size * part : size * (part + 1)]


def partial_kernel(groups, position, listed, regions, upstream, above, middle, below, out, shifts):
    tile_rows, channels, columns = upstream.shape
    fill_shifts(above, middle, below, shifts)

    @pl.loop(0, columns // LANES, unroll=8)
    def _(band):
        cells = unfolded(shifts, band, tile_rows)
        mask = first_mask(regions, listed, band, channels, tile_rows)
        store_partial(groups, position, band, side_by_side(upstream, band, tile_rows), cells, mask, out)


def partial_of(position, listed, regions, upstream, above, middle, below, places, groups):
    tile_rows, channels, columns = middle.shape
    rows = 9 * channels * channels // LANES
    return pl.pallas_call(
        functools.partial(partial_kernel, groups),
        out_shape=(
            jax.ShapeDtypeStruct((places, rows, LANES), BF16),
            jax.ShapeDtypeStruct((3, tile_rows + 2, channels, columns), BF16),
        ),
        in_specs=[SMEM, SMEM] + [VMEM] * 5,
        out_specs=(VMEM, VMEM),
        compiler_params=params(56),
        cost_estimate=cost(4 * 9 * channels * channels * columns * tile_rows, 8000000),
        name="partial_1",
    )(position, listed, regions, upstream, above, middle, below)


def carried_kernel(
    groups, position, listed, regions, cotangent, hidden, inner, from_above, from_below, shifts, carried, out
):
    tile_rows, channels, columns = hidden.shape

    @pl.loop(0, columns // LANES, unroll=8)
    def _(band):
        cells = unfolded(shifts, band, tile_rows)
        mask = first_mask(regions, listed, band, channels, tile_rows)
        back = []
        for row in range(tile_rows):
            value = inner[row, :, band_slice(band)]
            if row == 0:
                value = value + from_above[:, band_slice(band)].astype(F32)
            if row == tile_rows - 1:
                value = value + from_below[:, band_slice(band)].astype(F32)
            back.append(value)
        keep = side_by_side(hidden, band, tile_rows).astype(F32) > 0.0
        back = jnp.where(keep, jnp.concatenate(back, axis=1), 0.0)
        upstream = (side_by_side(cotangent, band, tile_rows).astype(F32) + back).astype(BF16)
        store_rows(carried, band, upstream)
        store_partial(groups, position, band, upstream, cells, mask, out)


def carried_of(
    position, listed, regions, cotangent, hidden, inner, from_above, from_below, shifts, places, groups
):
    tile_rows, channels, columns = hidden.shape
    rows = 9 * channels * channels // LANES
    return pl.pallas_call(
        functools.partial(carried_kernel, groups),
        out_shape=(
            jax.ShapeDtypeStruct(hidden.shape, BF16),
            jax.ShapeDtypeStruct((places, rows, LANES), BF16),
        ),
        in_specs=[SMEM, SMEM] + [VMEM] * 7,
        out_specs=(VMEM, VMEM),
        compiler_params=params(32),
        cost_estimate=cost(4 * 9 * channels * channels * columns * tile_rows, 7000000),
        name="carried_partial_0",
    )(position, listed, regions, cotangent, hidden, inner, from_above, from_below, shifts)


def spread_kernel(position, listed, regions, upstream, *rest):
    pieces, (inner, edges, total) = rest[:-3], rest[-3:]
    tile_rows, channels, columns = upstream.shape
    total[...] = jnp.zeros_like(total)

    @pl.loop(0, columns // LANES, unroll=8)
    def _(band):
        wide, last = band_weights(pieces, pieces[0].shape[0], position, band)
        mask = first_mask(regions, listed, band, channels, tile_rows)
        both = masked(side_by_side(upstream, band, tile_rows), mask)
        spread = jnp.concatenate([dot(wide, both, 0, 0), dot(last, both, 0, 0)], axis=0)
        lane = lax.broadcasted_iota(jnp.int32, (channels, LANES), 1)
        for target in range(tile_rows + 2):
            moved = []
            for shift_x in range(3):
                value = None
                for row in range(tile_rows):
                    shift_y = target - 1 - row + 1
                    if 0 <= shift_y <= 2:
                        tap = 3 * shift_y + shift_x
                        piece = spread[
                            channels * tap : channels * (tap + 1), LANES * row : LANES * (row + 1)
                        ]
                        value = piece if value is None else value + piece
                moved.append(value)
            left = pltpu.roll(moved[0], LANES - 1, 1)
            right = pltpu.roll(moved[2], 1, 1)
            centre = (
                moved[1]
                + jnp.where(lane == LANES - 1, 0.0, left)
                + jnp.where(lane == 0, 0.0, right)
            )
            total[target, :, band_slice(band)] += jnp.where(lane == LANES - 1, left, 0.0)
            total[target, :, band_slice(band + 1)] += centre
            total[target, :, band_slice(band + 2)] += jnp.where(lane == 0, right, 0.0)

    for row in range(tile_rows):
        inner[row] = total[row + 1, :, LANES : LANES + columns]
    edges[0] = total[0, :, LANES : LANES + columns].astype(BF16)
    edges[1] = total[tile_rows + 1, :, LANES : LANES + columns].astype(BF16)


def spread_of(position, listed, regions, upstream, kernels, name, room=32):
    tile_rows, channels, columns = upstream.shape
    return pl.pallas_call(
        spread_kernel,
        out_shape=(
            jax.ShapeDtypeStruct(upstream.shape, F32),
            jax.ShapeDtypeStruct((2, channels, columns), BF16),
        ),
        in_specs=[SMEM, SMEM] + [VMEM] * (2 + len(kernels)),
        out_specs=(VMEM, VMEM),
        scratch_shapes=[pltpu.VMEM((tile_rows + 2, channels, columns + 2 * LANES), F32)],
        compiler_params=params(room),
        cost_estimate=cost(4 * 9 * channels * channels * columns * tile_rows, 5000000),
        name=name,
    )(position, listed, regions, upstream, *kernels)


GY = ("far", "near")
PLANE = ("groups", "near")
ALL = ("groups", "far", "near")


def from_neighbours(upper, lower):
    count = lax.axis_size(GY)
    above = lax.ppermute(upper, GY, [(i, i + 1) for i in range(count - 1)])
    below = lax.ppermute(lower, GY, [(i + 1, i) for i in range(count - 1)])
    return above, below


def exchange(value, axes):
    return lax.all_to_all(value, axes, split_axis=0, concat_axis=0, tiled=True)


def after(first, value):
    return lax.optimization_barrier((*first, value))


def places_for(owner, owners, per_owner, content):
    order = jnp.arange(owner.shape[0], dtype=jnp.int32)
    earlier = (owner[:, None] == owner[None, :]) & (order[None, :] < order[:, None])
    position = owner * per_owner + jnp.sum(earlier.astype(jnp.int32), axis=-1)
    hits = position[None, :] == jnp.arange(owners * per_owner, dtype=jnp.int32)[:, None]
    wanted = jnp.max(jnp.where(hits, content[None, :], -1), axis=1)
    return position, wanted.reshape(owners, per_owner)


def body(field, cotangent, banks, region_map, tile_regions, bank_slot):
    col_bands = tile_regions.shape[0]
    groups, far, near = (lax.axis_size(axis) for axis in ALL)
    devices = far * near
    per_dev = banks.shape[1]
    slots_per = max(1, 2 * col_bands // devices)
    places = devices * slots_per
    listed = tile_regions.reshape(-1)
    bank_row = bank_slot[listed]
    holder = bank_row // per_dev
    local_row = bank_row % per_dev
    position, wanted = places_for(holder, devices, slots_per, local_row)
    my_group, my_far = lax.axis_index("groups"), lax.axis_index("far")

    cells = jnp.transpose(field, (1, 0, 2))
    upstream = jnp.transpose(cotangent, (1, 0, 2))
    last = cells.shape[0] - 1
    where = (position, listed, region_map)

    message = jnp.transpose(wanted.reshape(far, near, slots_per), (1, 0, 2))
    message = jnp.broadcast_to(message[None, None], (groups, far, near, far, slots_per))
    own_part = my_group.astype(jnp.int32).reshape(1)
    message = exchange(message.reshape(groups * devices, far * slots_per), ALL)
    message = message.reshape(groups, far, near, far, slots_per)
    mine = lax.dynamic_index_in_dim(message, my_group, 0, False)
    requested = lax.dynamic_index_in_dim(mine, my_far, 2, False).reshape(-1)
    asked = lax.dynamic_index_in_dim(message, my_far, 1, False).reshape(groups * near, far, slots_per)
    steps = jnp.arange(far, dtype=jnp.int32)
    asked = jnp.maximum(jnp.take(asked, (my_far - steps) % far, axis=1), 0)
    asked = asked.reshape(groups * near, far * slots_per)

    step = (my_far - holder // near) % far
    place = (holder % near * far + step) * slots_per + position % slots_per
    fetch = (place.astype(jnp.int32), listed, region_map)

    above, below = from_neighbours(cells[last], cells[0])
    turns = [[(k, (k + turn) % far) for k in range(far)] for turn in range(1, far)]
    whole = part_rows(groups)
    wire_a, wire_b = wire(own_part, banks, 1, groups, (64, whole - 64))
    (wire_zero,) = wire(own_part, banks, 0, groups, (whole,))

    def gathered(mine):
        return [mine] + [lax.ppermute(mine, "far", turn) for turn in turns]

    def fetched(buffers, name):
        arrived = exchange(pack(asked, buffers, name), PLANE)
        return arrived.reshape(groups, near * far * slots_per, *arrived.shape[1:])

    bank_a = gathered(wire_a)
    *bank_a, wire_b = after(bank_a, wire_b)
    bank_b = gathered(wire_b)
    bank_b[-1], above, below, wire_zero = after((bank_b[-1], above, below), wire_zero)
    bank_zero = gathered(wire_zero)
    kernel_one = [fetched(bank_a, "pack_1a"), fetched(bank_b, "pack_1b")]
    kernel_zero = [fetched(bank_zero, "pack_0")]
    shifts = shift(above, cells, below, "shift_0")
    shifts, upstream_one = after((shifts,), upstream)
    inner_one, edges_one = spread_of(*fetch, upstream_one, kernel_one, "spread_1")
    from_above, from_below = from_neighbours(edges_one[1], edges_one[0])
    hidden = conv(*fetch, cells, shifts, kernel_zero, "conv_0")
    hidden_above, hidden_below = from_neighbours(hidden[last], hidden[0])
    carried, partial_zero = carried_of(
        *where, upstream, hidden, inner_one, from_above, from_below, shifts, places, groups
    )
    hidden_above, hidden_below, partial_zero = after((hidden_above, hidden_below), partial_zero)
    around = (hidden_above, hidden, hidden_below)
    sent_zero = exchange(partial_zero, GY)
    inner_zero, edges_zero = spread_of(*fetch, carried, kernel_zero, "spread_0", 56)
    from_above, from_below = from_neighbours(edges_zero[1], edges_zero[0])
    partial_one, shifts_one = partial_of(*where, upstream, *around, places, groups)
    from_above, from_below, partial_one = after((from_above, from_below), partial_one)
    sent_one = exchange(partial_one, GY)
    refined = conv(*fetch, hidden, shifts_one, kernel_one, "conv_1")
    back = inner_zero.at[0].add(from_above.astype(F32)).at[last].add(from_below.astype(F32))
    input_grad = (carried.astype(F32) + jnp.where(cells > 0, back, 0.0)).astype(BF16)
    half = total_of(requested, sent_zero, banks, 0, groups)
    grad_banks = total_of(requested, sent_one, banks, 1, groups, half)
    return (jnp.transpose(refined, (1, 0, 2)), jnp.transpose(input_grad, (1, 0, 2)), grad_banks)


def solution(mesh):
    groups, devices = mesh.shape["groups"], mesh.shape["gy"]
    cut = Mesh(mesh.devices.reshape(groups, devices // NEAR, NEAR), ALL)
    return jax.shard_map(
        body,
        mesh=cut,
        in_specs=(
            P(None, ALL, None),
            P(None, ALL, None),
            P(None, GY, None),
            P(ALL, None),
            P(ALL, None),
            P("groups"),
        ),
        out_specs=(
            P(None, ALL, None),
            P(None, ALL, None),
            P("groups", GY, None),
        ),
        check_vma=False,
    )
```

```python
import functools

import jax
import jax.numpy as jnp
from jax import lax
from jax.experimental import pallas as pl
from jax.experimental.pallas import tpu as pltpu
from jax.sharding import Mesh
from jax.sharding import PartitionSpec as P

grad_unscale = 0.03125
F32 = jnp.float32
BF16 = jnp.bfloat16
LANES = 128
VMEM = pl.BlockSpec(memory_space=pltpu.VMEM)
SMEM = pl.BlockSpec(memory_space=pltpu.SMEM)
HBM = pl.BlockSpec(memory_space=pl.ANY)

NEAR = 4


def pairs_of(parts):
    return 4 // parts


def tail_of(parts):
    return 32 // parts


def part_rows(parts):
    return 64 * pairs_of(parts) + tail_of(parts)


def pair_start(pair, parts):
    return pair // pairs_of(parts) * part_rows(parts) + 64 * (pair % pairs_of(parts))


def tail_start(part, parts):
    return part * part_rows(parts) + 64 * pairs_of(parts)


def params(mib):
    return pltpu.CompilerParams(vmem_limit_bytes=mib * 2**20)


def cost(flops, moved):
    return pl.CostEstimate(flops=flops, bytes_accessed=moved, transcendentals=0)


def swap_halves(tile):
    return pltpu.roll(tile, LANES // 2, 1)


def low_half(tile):
    return lax.broadcasted_iota(jnp.int32, tile.shape, 1) < LANES // 2


def wire_kernel(parts, per_dev, rows, own_part, banks, *rest):
    outs, (natural, travel) = rest[:-2], rest[-2:]
    for part in range(parts):

        @pl.when(own_part[0] == part)
        def _(part=part):
            pairs = range(part * pairs_of(parts), (part + 1) * pairs_of(parts))
            half = tail_of(parts) // 2
            for chunk in [*range(64 * pairs[0], 64 * pairs[-1] + 64), *range(256, rows)]:
                tile = banks[0, :, chunk * LANES : (chunk + 1) * LANES].astype(F32)
                natural[pl.ds(chunk, per_dev, stride=rows), :] = tile

            @pl.loop(0, per_dev)
            def _(row):
                base = row * rows

                def blend(first, second, start, count):
                    first = natural[pl.ds(base + first, count), :]
                    second = natural[pl.ds(base + second, count), :]
                    even = jnp.where(low_half(first), first, swap_halves(second))
                    odd = jnp.where(low_half(first), swap_halves(first), second)
                    travel[pl.ds(start, count, stride=2), :] = even
                    travel[pl.ds(start + 1, count, stride=2), :] = odd

                for order, pair in enumerate(pairs):
                    blend(64 * pair, 64 * pair + 32, 64 * order, 32)
                blend(256 + part * half, 272 + part * half, 64 * len(pairs), half)
                start = 0
                for out in outs:
                    out[row] = travel[start : start + out.shape[1], :].astype(BF16)
                    start += out.shape[1]


def wire(own_part, banks, layer, parts, sizes):
    layers, per_dev, width = banks.shape
    rows = width // LANES
    return pl.pallas_call(
        functools.partial(wire_kernel, parts, per_dev, rows),
        grid=(1,),
        out_shape=[jax.ShapeDtypeStruct((per_dev, size, LANES), BF16) for size in sizes],
        in_specs=[SMEM, pl.BlockSpec((1, per_dev, width), lambda step: (layer, 0, 0))],
        out_specs=[pl.BlockSpec((per_dev, size, LANES), lambda step: (0, 0, 0)) for size in sizes],
        scratch_shapes=[
            pltpu.VMEM((per_dev * rows, LANES), F32),
            pltpu.VMEM((part_rows(parts), LANES), F32),
        ],
        compiler_params=params(24),
        cost_estimate=cost(10**6, 4 * per_dev * width),
        name=f"wire_{layer}",
    )(own_part, banks)


def pack_kernel(rows, *refs):
    buffers, out = refs[:-1], refs[-1]
    inner = rows.shape[1]
    slots = inner // len(buffers)

    @pl.loop(0, rows.shape[0])
    def _(target):
        for entry in range(inner):
            out[target * inner + entry] = buffers[entry // slots][rows[target, entry]]


def pack(rows, buffers, name):
    targets, inner = rows.shape
    shape = buffers[0].shape[1:]
    return pl.pallas_call(
        pack_kernel,
        out_shape=jax.ShapeDtypeStruct((targets * inner, *shape), BF16),
        in_specs=[SMEM] + [VMEM] * len(buffers),
        out_specs=VMEM,
        compiler_params=params(32),
        cost_estimate=cost(10**11, 4 * targets * inner * shape[0] * shape[1]),
        name=name,
    )(rows, *buffers)


def total_kernel(groups, per_dev, rows, requested, parts, *rest):
    out, total, natural = rest[-3:]
    total[...] = jnp.zeros_like(total)

    @pl.loop(0, parts.shape[0], unroll=8)
    def _(place):
        row = jnp.where(requested[place] < 0, per_dev, requested[place])
        total[pl.ds(pl.multiple_of(row * rows, 8), rows), :] += parts[place].astype(F32)

    @pl.loop(0, per_dev, unroll=4)
    def _(row):
        base = row * rows

        def split(start, count, first, second):
            even = total[pl.ds(base + start, count, stride=2), :] * grad_unscale
            odd = total[pl.ds(base + start + 1, count, stride=2), :] * grad_unscale
            natural[pl.ds(base + first, count), :] = jnp.where(low_half(even), even, swap_halves(odd))
            natural[pl.ds(base + second, count), :] = jnp.where(low_half(even), swap_halves(even), odd)

        for pair in range(4):
            split(pair_start(pair, groups), 32, 64 * pair, 64 * pair + 32)
        half = tail_of(groups) // 2
        for part in range(groups):
            split(tail_start(part, groups), half, 256 + part * half, 272 + part * half)

    for chunk in range(rows):
        out[0, :, chunk * LANES : (chunk + 1) * LANES] = natural[pl.ds(chunk, per_dev, stride=rows), :]


def total_of(requested, parts, banks, layer, groups, earlier=None):
    layers, per_dev, width = banks.shape
    rows = width // LANES
    places = requested.shape[0]
    args, specs = [requested, parts], [SMEM, pl.BlockSpec(parts.shape, lambda step: (0, 0, 0))]
    if earlier is not None:
        args.append(earlier)
        specs.append(HBM)
    return pl.pallas_call(
        functools.partial(total_kernel, groups, per_dev, rows),
        grid=(1,),
        out_shape=jax.ShapeDtypeStruct((layers, per_dev, width), F32),
        in_specs=specs,
        out_specs=pl.BlockSpec((1, per_dev, width), lambda step: (layer, 0, 0)),
        scratch_shapes=[
            pltpu.VMEM(((per_dev + 1) * rows, LANES), F32),
            pltpu.VMEM((per_dev * rows, LANES), F32),
        ],
        input_output_aliases={2: 0} if earlier is not None else {},
        compiler_params=params(32),
        cost_estimate=cost(1000000, 2 * places * width + 4 * per_dev * width),
        name=f"total_{layer}",
    )(*args)


def fill_shifts(above, middle, below, shifts):
    tile_rows, channels, columns = middle.shape
    step = 16

    @pl.loop(0, channels // step)
    def _(group):
        start = pl.multiple_of(group * step, step)
        for row in range(tile_rows + 2):
            if row == 0:
                cells = above[pl.ds(start, step), :]
            elif row == tile_rows + 1:
                cells = below[pl.ds(start, step), :]
            else:
                cells = middle[row - 1, pl.ds(start, step), :]
            cells = jnp.maximum(cells.astype(F32), 0.0)
            column = lax.broadcasted_iota(jnp.int32, cells.shape, 1)
            left = jnp.where(column == 0, 0.0, pltpu.roll(cells, 1, 1))
            right = jnp.where(column == columns - 1, 0.0, pltpu.roll(cells, columns - 1, 1))
            shifts[0, row, pl.ds(start, step), :] = left.astype(BF16)
            shifts[1, row, pl.ds(start, step), :] = cells.astype(BF16)
            shifts[2, row, pl.ds(start, step), :] = right.astype(BF16)


def shift(above, middle, below, name):
    tile_rows, channels, columns = middle.shape
    return pl.pallas_call(
        fill_shifts,
        out_shape=jax.ShapeDtypeStruct((3, tile_rows + 2, channels, columns), BF16),
        in_specs=[VMEM] * 3,
        out_specs=VMEM,
        compiler_params=params(32),
        cost_estimate=cost(10**7, 8 * tile_rows * channels * columns),
        name=name,
    )(above, middle, below)


def band_slice(band):
    return pl.ds(pl.multiple_of(band * LANES, LANES), LANES)


def unfolded(shifts, band, tile_rows):
    taps = []
    for shift_y in range(3):
        for shift_x in range(3):
            rows = [shifts[shift_x, shift_y + row, :, band_slice(band)] for row in range(tile_rows)]
            taps.append(jnp.concatenate(rows, axis=1))
    return jnp.concatenate(taps, axis=0)


def band_weights(pieces, groups, place_of, band):
    def rows_of(part, place, start, count):
        for piece in pieces:
            if start < piece.shape[2]:
                return piece.at[part, place][start : start + count, :]
            start -= piece.shape[2]

    wide, last = [], []
    tail = 64 * pairs_of(groups)
    for slot in range(2):
        place = place_of[2 * band + slot]
        blocks = [rows_of(part, place, start, 64) for part in range(groups) for start in range(0, tail, 64)]
        wide.append(jnp.concatenate(blocks, axis=1))
        rest = [rows_of(part, place, tail, tail_of(groups)) for part in range(groups)]
        rest = jnp.concatenate(rest, axis=0)
        last.extend([rest[:, :64], rest[:, 64:]])
    return jnp.concatenate(wide, axis=0), jnp.concatenate(last, axis=0)


def first_mask(regions, listed, band, channels, tile_rows):
    rows = [regions[row : row + 1, band_slice(band)] for row in range(tile_rows)]
    flat = jnp.concatenate(rows, axis=1)
    return jnp.broadcast_to(flat, (channels, flat.shape[1])) == listed[2 * band]


def masked(upstream, mask):
    wide = upstream.astype(F32)
    first = jnp.where(mask, wide, 0.0).astype(BF16)
    second = jnp.where(mask, 0.0, wide).astype(BF16)
    return jnp.concatenate([first, second], axis=0)


def side_by_side(cells, band, tile_rows):
    return jnp.concatenate([cells[row, :, band_slice(band)] for row in range(tile_rows)], axis=1)


def dot(left, right, left_dim, right_dim):
    return lax.dot_general(
        left, right, (((left_dim,), (right_dim,)), ((), ())), preferred_element_type=F32
    )


def conv_kernel(position, listed, regions, middle, shifts, *rest):
    pieces, out = rest[:-1], rest[-1]
    tile_rows, channels, columns = middle.shape

    @pl.loop(0, columns // LANES, unroll=8)
    def _(band):
        cells = unfolded(shifts, band, tile_rows)
        wide, last = band_weights(pieces, pieces[0].shape[0], position, band)
        both = dot(wide, cells[:512], 1, 0) + dot(last, cells[512:], 1, 0)
        mask = first_mask(regions, listed, band, channels, tile_rows)
        mixed = jnp.where(mask, both[:channels], both[channels:])
        for row in range(tile_rows):
            here = mixed[:, row * LANES : (row + 1) * LANES]
            here = here + middle[row, :, band_slice(band)].astype(F32)
            out[row, :, band_slice(band)] = here.astype(BF16)


def conv(position, listed, regions, middle, shifts, kernels, name, room=32):
    tile_rows, channels, columns = middle.shape
    return pl.pallas_call(
        conv_kernel,
        out_shape=jax.ShapeDtypeStruct(middle.shape, BF16),
        in_specs=[SMEM, SMEM] + [VMEM] * (3 + len(kernels)),
        out_specs=VMEM,
        compiler_params=params(room),
        cost_estimate=cost(4 * 9 * channels * channels * columns * tile_rows, 5000000),
        name=name,
    )(position, listed, regions, middle, shifts, *kernels)


def store_rows(out, band, cells):
    for row in range(out.shape[0]):
        out[row, :, band_slice(band)] = cells[:, row * LANES : (row + 1) * LANES]


def store_partial(groups, position, band, upstream, cells, mask, out):
    channels = upstream.shape[0]
    sums = dot(masked(upstream, mask), cells, 1, 1).astype(BF16)
    for slot in range(2):
        mine = sums[channels * slot : channels * (slot + 1)]
        there = out.at[position[2 * band + slot]]
        for pair in range(4):
            start = pair_start(pair, groups)
            there[start : start + 64, :] = mine[:, LANES * pair : LANES * (pair + 1)]
        rest = jnp.concatenate([mine[:32, 512:], mine[32:, 512:]], axis=1)
        size = tail_of(groups)
        for part in range(groups):
            start = tail_start(part, groups)
            there[start : start + size, :] = rest[size * part : size * (part + 1)]


def partial_kernel(groups, position, listed, regions, upstream, above, middle, below, out, shifts):
    tile_rows, channels, columns = upstream.shape
    fill_shifts(above, middle, below, shifts)

    @pl.loop(0, columns // LANES, unroll=8)
    def _(band):
        cells = unfolded(shifts, band, tile_rows)
        mask = first_mask(regions, listed, band, channels, tile_rows)
        store_partial(groups, position, band, side_by_side(upstream, band, tile_rows), cells, mask, out)


def partial_of(position, listed, regions, upstream, above, middle, below, places, groups):
    tile_rows, channels, columns = middle.shape
    rows = 9 * channels * channels // LANES
    return pl.pallas_call(
        functools.partial(partial_kernel, groups),
        out_shape=(
            jax.ShapeDtypeStruct((places, rows, LANES), BF16),
            jax.ShapeDtypeStruct((3, tile_rows + 2, channels, columns), BF16),
        ),
        in_specs=[SMEM, SMEM] + [VMEM] * 5,
        out_specs=(VMEM, VMEM),
        compiler_params=params(56),
        cost_estimate=cost(4 * 9 * channels * channels * columns * tile_rows, 8000000),
        name="partial_1",
    )(position, listed, regions, upstream, above, middle, below)


def carried_kernel(
    groups, position, listed, regions, cotangent, hidden, inner, from_above, from_below, shifts, carried, out
):
    tile_rows, channels, columns = hidden.shape

    @pl.loop(0, columns // LANES, unroll=8)
    def _(band):
        cells = unfolded(shifts, band, tile_rows)
        mask = first_mask(regions, listed, band, channels, tile_rows)
        back = []
        for row in range(tile_rows):
            value = inner[row, :, band_slice(band)]
            if row == 0:
                value = value + from_above[:, band_slice(band)].astype(F32)
            if row == tile_rows - 1:
                value = value + from_below[:, band_slice(band)].astype(F32)
            back.append(value)
        keep = side_by_side(hidden, band, tile_rows).astype(F32) > 0.0
        back = jnp.where(keep, jnp.concatenate(back, axis=1), 0.0)
        upstream = (side_by_side(cotangent, band, tile_rows).astype(F32) + back).astype(BF16)
        store_rows(carried, band, upstream)
        store_partial(groups, position, band, upstream, cells, mask, out)


def carried_of(
    position, listed, regions, cotangent, hidden, inner, from_above, from_below, shifts, places, groups
):
    tile_rows, channels, columns = hidden.shape
    rows = 9 * channels * channels // LANES
    return pl.pallas_call(
        functools.partial(carried_kernel, groups),
        out_shape=(
            jax.ShapeDtypeStruct(hidden.shape, BF16),
            jax.ShapeDtypeStruct((places, rows, LANES), BF16),
        ),
        in_specs=[SMEM, SMEM] + [VMEM] * 7,
        out_specs=(VMEM, VMEM),
        compiler_params=params(32),
        cost_estimate=cost(4 * 9 * channels * channels * columns * tile_rows, 7000000),
        name="carried_partial_0",
    )(position, listed, regions, cotangent, hidden, inner, from_above, from_below, shifts)


def spread_kernel(position, listed, regions, upstream, *rest):
    pieces, (inner, edges, total) = rest[:-3], rest[-3:]
    tile_rows, channels, columns = upstream.shape
    total[...] = jnp.zeros_like(total)

    @pl.loop(0, columns // LANES, unroll=8)
    def _(band):
        wide, last = band_weights(pieces, pieces[0].shape[0], position, band)
        mask = first_mask(regions, listed, band, channels, tile_rows)
        both = masked(side_by_side(upstream, band, tile_rows), mask)
        spread = jnp.concatenate([dot(wide, both, 0, 0), dot(last, both, 0, 0)], axis=0)
        lane = lax.broadcasted_iota(jnp.int32, (channels, LANES), 1)
        for target in range(tile_rows + 2):
            moved = []
            for shift_x in range(3):
                value = None
                for row in range(tile_rows):
                    shift_y = target - 1 - row + 1
                    if 0 <= shift_y <= 2:
                        tap = 3 * shift_y + shift_x
                        piece = spread[
                            channels * tap : channels * (tap + 1), LANES * row : LANES * (row + 1)
                        ]
                        value = piece if value is None else value + piece
                moved.append(value)
            left = pltpu.roll(moved[0], LANES - 1, 1)
            right = pltpu.roll(moved[2], 1, 1)
            centre = (
                moved[1]
                + jnp.where(lane == LANES - 1, 0.0, left)
                + jnp.where(lane == 0, 0.0, right)
            )
            total[target, :, band_slice(band)] += jnp.where(lane == LANES - 1, left, 0.0)
            total[target, :, band_slice(band + 1)] += centre
            total[target, :, band_slice(band + 2)] += jnp.where(lane == 0, right, 0.0)

    for row in range(tile_rows):
        inner[row] = total[row + 1, :, LANES : LANES + columns]
    edges[0] = total[0, :, LANES : LANES + columns].astype(BF16)
    edges[1] = total[tile_rows + 1, :, LANES : LANES + columns].astype(BF16)


def spread_of(position, listed, regions, upstream, kernels, name, room=32):
    tile_rows, channels, columns = upstream.shape
    return pl.pallas_call(
        spread_kernel,
        out_shape=(
            jax.ShapeDtypeStruct(upstream.shape, F32),
            jax.ShapeDtypeStruct((2, channels, columns), BF16),
        ),
        in_specs=[SMEM, SMEM] + [VMEM] * (2 + len(kernels)),
        out_specs=(VMEM, VMEM),
        scratch_shapes=[pltpu.VMEM((tile_rows + 2, channels, columns + 2 * LANES), F32)],
        compiler_params=params(room),
        cost_estimate=cost(4 * 9 * channels * channels * columns * tile_rows, 5000000),
        name=name,
    )(position, listed, regions, upstream, *kernels)


GY = ("far", "near")
PLANE = ("groups", "near")
ALL = ("groups", "far", "near")


def from_neighbours(upper, lower):
    count = lax.axis_size(GY)
    above = lax.ppermute(upper, GY, [(i, i + 1) for i in range(count - 1)])
    below = lax.ppermute(lower, GY, [(i + 1, i) for i in range(count - 1)])
    return above, below


def exchange(value, axes):
    return lax.all_to_all(value, axes, split_axis=0, concat_axis=0, tiled=True)


def after(first, value):
    return lax.optimization_barrier((*first, value))


def places_for(owner, owners, per_owner, content):
    order = jnp.arange(owner.shape[0], dtype=jnp.int32)
    earlier = (owner[:, None] == owner[None, :]) & (order[None, :] < order[:, None])
    position = owner * per_owner + jnp.sum(earlier.astype(jnp.int32), axis=-1)
    hits = position[None, :] == jnp.arange(owners * per_owner, dtype=jnp.int32)[:, None]
    wanted = jnp.max(jnp.where(hits, content[None, :], -1), axis=1)
    return position, wanted.reshape(owners, per_owner)


def body(field, cotangent, banks, region_map, tile_regions, bank_slot):
    col_bands = tile_regions.shape[0]
    groups, far, near = (lax.axis_size(axis) for axis in ALL)
    devices = far * near
    per_dev = banks.shape[1]
    slots_per = max(1, 2 * col_bands // devices)
    places = devices * slots_per
    listed = tile_regions.reshape(-1)
    bank_row = bank_slot[listed]
    holder = bank_row // per_dev
    local_row = bank_row % per_dev
    position, wanted = places_for(holder, devices, slots_per, local_row)
    my_group, my_far = lax.axis_index("groups"), lax.axis_index("far")

    cells = jnp.transpose(field, (1, 0, 2))
    upstream = jnp.transpose(cotangent, (1, 0, 2))
    last = cells.shape[0] - 1
    where = (position, listed, region_map)

    message = jnp.transpose(wanted.reshape(far, near, slots_per), (1, 0, 2))
    message = jnp.broadcast_to(message[None, None], (groups, far, near, far, slots_per))
    own_part = my_group.astype(jnp.int32).reshape(1)
    message = exchange(message.reshape(groups * devices, far * slots_per), ALL)
    message = message.reshape(groups, far, near, far, slots_per)
    mine = lax.dynamic_index_in_dim(message, my_group, 0, False)
    requested = lax.dynamic_index_in_dim(mine, my_far, 2, False).reshape(-1)
    asked = lax.dynamic_index_in_dim(message, my_far, 1, False).reshape(groups * near, far, slots_per)
    steps = jnp.arange(far, dtype=jnp.int32)
    asked = jnp.maximum(jnp.take(asked, (my_far - steps) % far, axis=1), 0)
    asked = asked.reshape(groups * near, far * slots_per)

    step = (my_far - holder // near) % far
    place = (holder % near * far + step) * slots_per + position % slots_per
    fetch = (place.astype(jnp.int32), listed, region_map)

    above, below = from_neighbours(cells[last], cells[0])
    turns = [[(k, (k + turn) % far) for k in range(far)] for turn in range(1, far)]
    whole = part_rows(groups)
    wire_a, wire_b = wire(own_part, banks, 1, groups, (64, whole - 64))
    (wire_zero,) = wire(own_part, banks, 0, groups, (whole,))

    def gathered(mine):
        return [mine] + [lax.ppermute(mine, "far", turn) for turn in turns]

    def fetched(buffers, name):
        arrived = exchange(pack(asked, buffers, name), PLANE)
        return arrived.reshape(groups, near * far * slots_per, *arrived.shape[1:])

    bank_a = gathered(wire_a)
    *bank_a, wire_b = after(bank_a, wire_b)
    bank_b = gathered(wire_b)
    bank_b[-1], above, below, wire_zero = after((bank_b[-1], above, below), wire_zero)
    bank_zero = gathered(wire_zero)
    kernel_one = [fetched(bank_a, "pack_1a"), fetched(bank_b, "pack_1b")]
    kernel_zero = [fetched(bank_zero, "pack_0")]
    shifts = shift(above, cells, below, "shift_0")
    shifts, upstream_one = after((shifts,), upstream)
    inner_one, edges_one = spread_of(*fetch, upstream_one, kernel_one, "spread_1")
    from_above, from_below = from_neighbours(edges_one[1], edges_one[0])
    hidden = conv(*fetch, cells, shifts, kernel_zero, "conv_0")
    hidden_above, hidden_below = from_neighbours(hidden[last], hidden[0])
    carried, partial_zero = carried_of(
        *where, upstream, hidden, inner_one, from_above, from_below, shifts, places, groups
    )
    hidden_above, hidden_below, partial_zero = after((hidden_above, hidden_below), partial_zero)
    around = (hidden_above, hidden, hidden_below)
    sent_zero = exchange(partial_zero, GY)
    inner_zero, edges_zero = spread_of(*fetch, carried, kernel_zero, "spread_0", 56)
    from_above, from_below = from_neighbours(edges_zero[1], edges_zero[0])
    partial_one, shifts_one = partial_of(*where, upstream, *around, places, groups)
    from_above, from_below, partial_one = after((from_above, from_below), partial_one)
    sent_one = exchange(partial_one, GY)
    refined = conv(*fetch, hidden, shifts_one, kernel_one, "conv_1")
    back = inner_zero.at[0].add(from_above.astype(F32)).at[last].add(from_below.astype(F32))
    input_grad = (carried.astype(F32) + jnp.where(cells > 0, back, 0.0)).astype(BF16)
    half = total_of(requested, sent_zero, banks, 0, groups)
    grad_banks = total_of(requested, sent_one, banks, 1, groups, half)
    return (jnp.transpose(refined, (1, 0, 2)), jnp.transpose(input_grad, (1, 0, 2)), grad_banks)


def solution(mesh):
    groups, devices = mesh.shape["groups"], mesh.shape["gy"]
    cut = Mesh(mesh.devices.reshape(groups, devices // NEAR, NEAR), ALL)
    return jax.shard_map(
        body,
        mesh=cut,
        in_specs=(
            P(None, ALL, None),
            P(None, ALL, None),
            P(None, GY, None),
            P(ALL, None),
            P(ALL, None),
            P("groups"),
        ),
        out_specs=(
            P(None, ALL, None),
            P(None, ALL, None),
            P("groups", GY, None),
        ),
        check_vma=False,
    )
```
